32 devices in a mesh: pair: 8 (over z, x), win: 4 (over y, core).
Axes of the slice: x: 2, y: 2, z: 4, core: 2. Of those that a mesh axis runs over, the one named last changes fastest.
Arguments:
- spectra: bfloat16 [32, 2, 384, 2048], P(None, None, 'win', 'pair'), may hold values from -6 to 6
- channel_order: int32 [8, 256], P('pair'), may hold values from 0 to 255, each once within a row
- partners: int32 [4, 8], replicated, may hold values from 0 to 7, as said below
Outputs:
- stacks: float32 [8, 256, 4, 16, 256], P('pair', 'win')
The draws below stay inside these ranges and needn't reach their ends.
Inputs may be any that keep to these rules, and one draw needn't show every extreme that they name: For every round r and block b, partners[r, b] differs from b and partners[r, partners[r, b]] = b; no two rounds match the same two blocks. `channel_order`: each row lists every slot once.
All inputs are finite; a program needn't handle non-finite values.
Results may differ from the reference program's by a relative error of at most 0.004.
Values may be sent and summed in bfloat16 or wider, within the bound.
A program may use at most 128 MiB of HBM per device.

```python
import math
import jax
import jax.numpy as jnp
from jax import lax

CH = 256
NF = 32
LAGS = 16
ROUNDS = 4
BLOCKS = 8
WINDOWS = 384
CHANNELS = 2048


def draw_partners(key, part):
    key = jax.random.fold_in(key, 11)
    key_pick, key_label = jax.random.split(key)
    fixed_block = BLOCKS - 1
    chosen = jax.random.permutation(key_pick, fixed_block)[:ROUNDS].astype(jnp.int32)
    relabel = jax.random.permutation(key_label, BLOCKS).astype(jnp.int32)
    block_ids = jnp.arange(BLOCKS, dtype=jnp.int32)[None, :]
    chosen_col = chosen[:, None]
    circle_mate = jnp.where(block_ids == fixed_block, chosen_col, jnp.where(block_ids == chosen_col, fixed_block, (2 * chosen_col - block_ids) % fixed_block))
    result = jnp.zeros((ROUNDS, BLOCKS), jnp.int32)
    return result.at[:, relabel].set(relabel[circle_mate])


def steps_of(key, extent, pieces, least, top_value):
    factor_of = 1.0
    for dim, parts in pieces:
        heights = jax.random.uniform(jax.random.fold_in(jax.random.fold_in(key, 6), dim), (parts,), jnp.float32, least / len(pieces), top_value / len(pieces))
        factor_of = factor_of * jnp.repeat(jnp.exp(heights), extent[dim] // parts).reshape((-1,) + (1,) * (len(extent) - 1 - dim))
    return factor_of


def noise(stream_key, shape, spread, reach, cuts=(), held_as=jnp.bfloat16):
    array = jax.random.normal(stream_key, shape, jnp.float32) * spread
    if len(cuts) > 0:
        array = steps_of(stream_key, shape, cuts, -0.22, 0.18) * array
    return jnp.clip(array, min=-reach, max=reach).astype(held_as)


def setup_inputs(seed: int = 0) -> dict:
    keys = jax.random.split(jax.random.key(seed), 4)
    return {
        "spectra": noise(keys[0], (NF, 2, WINDOWS, CHANNELS), 1.0, 6.0, ((2, 4), (3, 8))),
        "channel_order": jax.vmap(lambda own: jax.random.permutation(own, CH))(jax.random.split(keys[1], BLOCKS)).reshape((BLOCKS, CH)).astype(jnp.int32),
        "partners": draw_partners(jax.random.fold_in(keys[3], 71), 0),
    }


def whiten(spectra):
    values = spectra.astype(jnp.float32)
    band_power = values[:, 0] * values[:, 0] + values[:, 1] * values[:, 1]
    num_bins = band_power.shape[0]
    padded = jnp.pad(band_power, ((2, 2), (0, 0), (0, 0)))
    band_total = padded[0:num_bins] + padded[1:num_bins + 1] + padded[2:num_bins + 2] + padded[3:num_bins + 3] + padded[4:num_bins + 4]
    bin_index = jnp.arange(num_bins, dtype=jnp.int32)
    counts = (jnp.minimum(bin_index + 2, num_bins - 1) - jnp.maximum(bin_index - 2, 0) + 1).astype(jnp.float32)
    band_mean = band_total / counts[:, None, None]
    inv_scale = 1.0 / jnp.maximum(jnp.sqrt(band_mean), 0.5)
    return (values * inv_scale[:, None]).astype(jnp.bfloat16)

def make_table(num_bins, num_lags, window_total):
    bin_freq = jnp.arange(num_bins, dtype=jnp.float32)[:, None]
    lag_index = (jnp.arange(num_lags, dtype=jnp.int32) - num_lags // 2).astype(jnp.float32)[None, :]
    phase_angle = math.pi * bin_freq * lag_index / num_bins
    norm_factor = 1.0 / math.sqrt(window_total * num_bins)
    return jnp.concatenate([jnp.cos(phase_angle), -jnp.sin(phase_angle)], 0) * norm_factor

def correlate(own_block, mate_block, lag_table):
    num_bins, _, num_windows, num_cols = own_block.shape
    left_rows = own_block.astype(jnp.float32).reshape(num_bins, 2 * num_windows, num_cols)
    mate_float = mate_block.astype(jnp.float32)
    right_real = mate_float.reshape(num_bins, 2 * num_windows, num_cols)
    right_turned = jnp.concatenate([mate_float[:, 1], -mate_float[:, 0]], axis=1)
    cross_real = jnp.einsum('fki,fkj->fij', left_rows, right_real, precision=lax.Precision.HIGHEST)
    cross_imag = jnp.einsum('fki,fkj->fij', left_rows, right_turned, precision=lax.Precision.HIGHEST)
    stacked = jnp.concatenate([cross_real, cross_imag], 0)
    return jnp.einsum('gl,gij->ilj', lag_table, stacked, precision=lax.Precision.HIGHEST)

def reference(spectra, channel_order, partners):
    whitened = whiten(spectra)
    blocks = whitened.reshape(NF, 2, WINDOWS, BLOCKS, CH)
    blocks = jnp.moveaxis(blocks, 3, 0)
    blocks = jax.vmap(lambda block_data, order_row: jnp.take(block_data, order_row, axis=3))(blocks, channel_order)
    lag_table = make_table(NF, LAGS, WINDOWS)

    def one_block(block_id):
        own_block = lax.dynamic_index_in_dim(blocks, block_id, 0, keepdims=False)
        results = []
        for turn_index in range(ROUNDS):
            mate_id = partners[turn_index, block_id].astype(jnp.int32)
            mate_block = lax.dynamic_index_in_dim(blocks, mate_id, 0, keepdims=False)
            results.append(correlate(own_block, mate_block, lag_table))
        return jnp.stack(results, 1)
    return lax.map(one_block, jnp.arange(BLOCKS, dtype=jnp.int32))
```

```python
import functools
import math

import jax
import jax.numpy as jnp
from jax import lax
from jax.experimental import pallas as pl
from jax.experimental.pallas import tpu as pltpu
from jax.sharding import PartitionSpec as P

LAGS = 16
ROUNDS = 4
GROUP = 16
BF = jnp.bfloat16
F32 = jnp.float32


def make_table(num_bins, num_lags, window_total):
    bin_freq = jnp.arange(num_bins, dtype=F32)[:, None]
    lag_index = (jnp.arange(num_lags, dtype=jnp.int32) - num_lags // 2).astype(F32)[None, :]
    phase_angle = math.pi * bin_freq * lag_index / num_bins
    norm_factor = 1.0 / math.sqrt(window_total * num_bins)
    return jnp.concatenate([jnp.cos(phase_angle), -jnp.sin(phase_angle)], 0) * norm_factor


def whiten_kernel(spec_ref, order_ref, own_ref, lhs_ref, power):
    nf, _, nw, nc = spec_ref.shape
    zero = jnp.zeros((nw, nc), F32)
    for edge in (0, 1, nf + 2, nf + 3):
        power[edge] = zero

    def square(f, carry):
        re = spec_ref[f, 0].astype(F32)
        im = spec_ref[f, 1].astype(F32)
        power[f + 2] = re * re + im * im
        return carry

    lax.fori_loop(0, nf, square, 0)
    rows = lax.broadcasted_iota(jnp.int32, (nc, nc), 0)
    cols = lax.broadcasted_iota(jnp.int32, (nc, nc), 1)
    pick = (rows == order_ref[...]).astype(F32).astype(BF)
    eye = (rows == cols).astype(F32).astype(BF)

    def scale(f, carry):
        total = power[f] + power[f + 1] + power[f + 2] + power[f + 3] + power[f + 4]
        count = jnp.minimum(f + 2, nf - 1) - jnp.maximum(f - 2, 0) + 1
        mean = total / count.astype(F32)
        inv = 1.0 / jnp.maximum(jnp.sqrt(mean), 0.5)
        white = jnp.concatenate(
            [
                (spec_ref[f, 0].astype(F32) * inv).astype(BF),
                (spec_ref[f, 1].astype(F32) * inv).astype(BF),
            ],
            0,
        )
        own = jnp.dot(white, pick, preferred_element_type=F32).astype(BF)
        own_ref[f] = own
        turned = lax.dot_general(eye, own, (((1,), (1,)), ((), ())), preferred_element_type=F32)
        lhs_ref[f] = turned.astype(BF)
        return carry

    lax.fori_loop(0, nf, scale, 0)


def whiten(spectra, order):
    nf, _, nw, nc = spectra.shape
    vmem = pl.BlockSpec(memory_space=pltpu.VMEM)
    return pl.pallas_call(
        whiten_kernel,
        out_shape=(
            jax.ShapeDtypeStruct((nf, 2 * nw, nc), BF),
            jax.ShapeDtypeStruct((nf, nc, 2 * nw), BF),
        ),
        in_specs=[vmem, vmem],
        out_specs=(vmem, vmem),
        scratch_shapes=[pltpu.VMEM((nf + 4, nw, nc), F32)],
        compiler_params=pltpu.CompilerParams(vmem_limit_bytes=40 * 2**20),
        name="whiten",
    )(spectra, order)


def corr_kernel(info_ref, lhs_ref, table_ref, *refs):
    mates = refs[:-5]
    keep_ref, send_ref, mate, cross, sem = refs[-5:]
    nf, nk, nc = mate.shape
    nw = nk // 2
    slot, core, row = info_ref[0], info_ref[1], info_ref[2]
    for s, ref in enumerate(mates):

        @pl.when(slot == s)
        def _(ref=ref):
            pltpu.make_async_copy(ref, mate, sem).start()

    pltpu.make_async_copy(mates[0], mate, sem).wait()

    def one_bin(f, carry):
        right = mate[f]
        turned = jnp.concatenate([right[nw:], -right[:nw]], 0)
        left = lhs_ref[f]
        cross[f] = jnp.dot(left, right, preferred_element_type=F32).astype(BF)
        cross[nf + f] = jnp.dot(left, turned, preferred_element_type=F32).astype(BF)
        return carry

    lax.fori_loop(0, nf, one_bin, 0)
    share = keep_ref.shape[1]
    per = share // GROUP

    def one_group(step, carry):
        half, u = step // per, step % per
        for other, out_ref in ((0, keep_ref), (1, send_ref)):
            owner = lax.rem(row + half, 2) * 2 + lax.rem(core + other, 2)
            start = pl.multiple_of(owner * share + u * GROUP, GROUP)
            right = cross[:, pl.ds(start, GROUP), :].reshape(2 * nf * GROUP, nc)
            lags = jnp.dot(table_ref[...], right, preferred_element_type=F32)
            at = pl.multiple_of(u * GROUP, GROUP)
            out_ref[half, pl.ds(at, GROUP)] = lags.reshape(GROUP, LAGS, nc).astype(out_ref.dtype)
        return carry

    lax.fori_loop(0, 2 * per, one_group, 0)


def correlate(info, lhs, table, mates):
    nf, nc, nk = lhs.shape
    vmem = pl.BlockSpec(memory_space=pltpu.VMEM)
    return pl.pallas_call(
        corr_kernel,
        out_shape=(
            jax.ShapeDtypeStruct((2, nc // 4, LAGS, nc), F32),
            jax.ShapeDtypeStruct((2, nc // 4, LAGS, nc), BF),
        ),
        in_specs=[pl.BlockSpec(memory_space=pltpu.SMEM), vmem, vmem]
        + [pl.BlockSpec(memory_space=pl.ANY)] * len(mates),
        out_specs=(vmem, vmem),
        scratch_shapes=[
            pltpu.VMEM((nf, nk, nc), BF),
            pltpu.VMEM((2 * nf, nc, nc), BF),
            pltpu.SemaphoreType.DMA,
        ],
        cost_estimate=pl.CostEstimate(
            flops=8_000_000_000, bytes_accessed=12_000_000, transcendentals=0
        ),
        compiler_params=pltpu.CompilerParams(vmem_limit_bytes=40 * 2**20),
        name="correlate",
    )(info, lhs, table, *mates)


def gather_blocks(own, blocks):
    chain = blocks // 2
    got = {}

    def send(block, pairs):
        return lax.ppermute(block, "pair", pairs)

    def chain_pairs(step, depth):
        links = []
        for c in range(chain):
            src = c + step
            if 0 <= c + step * depth < chain:
                links += [(2 * src + x, 2 * c + x) for x in range(2)]
        return links

    def swap_pairs(reach):
        return [
            (2 * c + x, 2 * c + 1 - x)
            for c in range(chain)
            if 0 <= c + reach < chain
            for x in range(2)
        ]

    got[(0, 1)] = send(own, swap_pairs(0))
    for depth in range(1, chain):
        for step in (1, -1):
            before = own if depth == 1 else got[(step * (depth - 1), 0)]
            got[(step * depth, 0)] = send(before, chain_pairs(step, depth))
    for depth in range(1, chain):
        for step in (1, -1):
            got[(step * depth, 1)] = send(got[(step * depth, 0)], swap_pairs(step * depth))
    return got


ARRIVAL = [(0, 1), (1, 0), (-1, 0), (2, 0), (-2, 0), (1, 1), (-1, 1)]
ARRIVAL += [(3, 0), (-3, 0), (2, 1), (-2, 1), (3, 1), (-3, 1)]
READY = (7, 9, 11, 13)


def local(spectra, channel_order, partners):
    num_blocks = lax.axis_size("pair")
    win_count = lax.axis_size("win")
    nf, _, nw, nc = spectra.shape
    table = make_table(nf, LAGS, nw * win_count)
    spread = (
        table.T[None, :, :, None] * jnp.eye(GROUP, dtype=F32)[:, None, None, :]
    ).reshape(GROUP * LAGS, 2 * nf * GROUP).astype(BF)
    own, lhs = whiten(spectra, channel_order)
    me = lax.axis_index("pair")
    win = lax.axis_index("win")
    row, core = win // 2, win % 2
    mine = partners[:, me]
    results = []
    if num_blocks == 8:
        got = gather_blocks(own, num_blocks)
        reach = mine // 2 - me // 2
        column = jnp.abs(mine % 2 - me % 2)
        rank = jnp.zeros_like(mine)
        for index, (step, other) in enumerate(ARRIVAL):
            rank = jnp.where((reach == step) & (column == other), index, rank)
        place = jnp.sum((rank[None, :] < rank[:, None]).astype(jnp.int32), 1)
    else:
        place = None
        turned = lax.all_to_all(
            own.reshape(num_blocks, -1), "pair", split_axis=0, concat_axis=0, tiled=True
        )
    for turn in range(ROUNDS):
        if place is None:
            arranged = jnp.take(turned, partners[turn], axis=0)
            received = lax.all_to_all(arranged, "pair", split_axis=0, concat_axis=0, tiled=True)
            mates, slot = [received.reshape(own.shape)], jnp.int32(0)
        else:
            mates = [got[key] for key in ARRIVAL[: READY[turn]]]
            slot = jnp.sum(jnp.where(place == turn, rank, 0))
        info = jnp.stack([slot, core, row]).astype(jnp.int32)
        keep, give = correlate(info, lhs, spread, mates)
        beside = lax.ppermute(give, "win", [(w, w ^ 1) for w in range(win_count)])
        passed = (keep[1] + beside[1].astype(F32)).astype(BF)
        across = lax.ppermute(passed, "win", [(w, w ^ 2) for w in range(win_count)])
        results.append(keep[0] + beside[0].astype(F32) + across.astype(F32))
    if place is None:
        return jnp.stack(results, 1)[None]
    ordered = []
    for turn in range(ROUNDS):
        at = place[turn]
        value = results[ROUNDS - 1]
        for k in range(ROUNDS - 1):
            value = jnp.where(at == k, results[k], value)
        ordered.append(value)
    return jnp.stack(ordered, 1)[None]


def solution(mesh):
    return jax.shard_map(
        local,
        mesh=mesh,
        in_specs=(P(None, None, "win", "pair"), P("pair", None), P()),
        out_specs=P("pair", "win", None, None, None),
        check_vma=False,
    )
```

```python
import math

import jax
import jax.numpy as jnp
from jax import lax
from jax.experimental import pallas as pl
from jax.experimental.pallas import tpu as pltpu
from jax.sharding import PartitionSpec as P

LAGS = 16
ROUNDS = 4
GROUP = 16
BF = jnp.bfloat16
F32 = jnp.float32


def make_table(num_bins, num_lags, window_total):
    bin_freq = jnp.arange(num_bins, dtype=F32)[:, None]
    lag_index = (jnp.arange(num_lags, dtype=jnp.int32) - num_lags // 2).astype(F32)[None, :]
    phase_angle = math.pi * bin_freq * lag_index / num_bins
    norm_factor = 1.0 / math.sqrt(window_total * num_bins)
    return jnp.concatenate([jnp.cos(phase_angle), -jnp.sin(phase_angle)], 0) * norm_factor


def whiten_kernel(spec_ref, order_ref, own_ref, lhs_ref, power):
    nf, _, nw, nc = spec_ref.shape
    zero = jnp.zeros((nw, nc), F32)
    for edge in (0, 1, nf + 2, nf + 3):
        power[edge] = zero

    def square(f, carry):
        re = spec_ref[f, 0].astype(F32)
        im = spec_ref[f, 1].astype(F32)
        power[f + 2] = re * re + im * im
        return carry

    lax.fori_loop(0, nf, square, 0)
    rows = lax.broadcasted_iota(jnp.int32, (nc, nc), 0)
    cols = lax.broadcasted_iota(jnp.int32, (nc, nc), 1)
    pick = (rows == order_ref[...]).astype(F32).astype(BF)
    eye = (rows == cols).astype(F32).astype(BF)

    def scale(f, carry):
        total = power[f] + power[f + 1] + power[f + 2] + power[f + 3] + power[f + 4]
        count = jnp.minimum(f + 2, nf - 1) - jnp.maximum(f - 2, 0) + 1
        mean = total / count.astype(F32)
        inv = 1.0 / jnp.maximum(jnp.sqrt(mean), 0.5)
        white = jnp.concatenate(
            [
                (spec_ref[f, 0].astype(F32) * inv).astype(BF),
                (spec_ref[f, 1].astype(F32) * inv).astype(BF),
            ],
            0,
        )
        own = jnp.dot(white, pick, preferred_element_type=F32).astype(BF)
        own_ref[f] = own
        turned = lax.dot_general(eye, own, (((1,), (1,)), ((), ())), preferred_element_type=F32)
        lhs_ref[f] = turned.astype(BF)
        return carry

    lax.fori_loop(0, nf, scale, 0)


def whiten(spectra, order):
    nf, _, nw, nc = spectra.shape
    vmem = pl.BlockSpec(memory_space=pltpu.VMEM)
    return pl.pallas_call(
        whiten_kernel,
        out_shape=(
            jax.ShapeDtypeStruct((nf, 2 * nw, nc), BF),
            jax.ShapeDtypeStruct((nf, nc, 2 * nw), BF),
        ),
        in_specs=[vmem, vmem],
        out_specs=(vmem, vmem),
        scratch_shapes=[pltpu.VMEM((nf + 4, nw, nc), F32)],
        compiler_params=pltpu.CompilerParams(vmem_limit_bytes=40 * 2**20),
        name="whiten",
    )(spectra, order)


def corr_kernel(info_ref, lhs_ref, table_ref, *refs):
    mates = refs[:-5]
    keep_ref, send_ref, mate, cross, sem = refs[-5:]
    nf, nk, nc = mate.shape
    nw = nk // 2
    slot, core, row = info_ref[0], info_ref[1], info_ref[2]
    for s, ref in enumerate(mates):

        @pl.when(slot == s)
        def _(ref=ref):
            pltpu.make_async_copy(ref, mate, sem).start()

    pltpu.make_async_copy(mates[0], mate, sem).wait()

    def one_bin(f, carry):
        right = mate[f]
        turned = jnp.concatenate([right[nw:], -right[:nw]], 0)
        left = lhs_ref[f]
        cross[f] = jnp.dot(left, right, preferred_element_type=F32).astype(BF)
        cross[nf + f] = jnp.dot(left, turned, preferred_element_type=F32).astype(BF)
        return carry

    lax.fori_loop(0, nf, one_bin, 0)
    share = keep_ref.shape[1]
    per = share // GROUP

    def one_group(step, carry):
        half, u = step // per, step % per
        for other, out_ref in ((0, keep_ref), (1, send_ref)):
            owner = lax.rem(row + half, 2) * 2 + lax.rem(core + other, 2)
            start = pl.multiple_of(owner * share + u * GROUP, GROUP)
            right = cross[:, pl.ds(start, GROUP), :].reshape(2 * nf * GROUP, nc)
            lags = jnp.dot(table_ref[...], right, preferred_element_type=F32)
            at = pl.multiple_of(u * GROUP, GROUP)
            out_ref[half, pl.ds(at, GROUP)] = lags.reshape(GROUP, LAGS, nc).astype(out_ref.dtype)
        return carry

    lax.fori_loop(0, 2 * per, one_group, 0)


def correlate(info, lhs, table, mates):
    nf, nc, nk = lhs.shape
    vmem = pl.BlockSpec(memory_space=pltpu.VMEM)
    return pl.pallas_call(
        corr_kernel,
        out_shape=(
            jax.ShapeDtypeStruct((2, nc // 4, LAGS, nc), F32),
            jax.ShapeDtypeStruct((2, nc // 4, LAGS, nc), BF),
        ),
        in_specs=[pl.BlockSpec(memory_space=pltpu.SMEM), vmem, vmem]
        + [pl.BlockSpec(memory_space=pl.ANY)] * len(mates),
        out_specs=(vmem, vmem),
        scratch_shapes=[
            pltpu.VMEM((nf, nk, nc), BF),
            pltpu.VMEM((2 * nf, nc, nc), BF),
            pltpu.SemaphoreType.DMA,
        ],
        cost_estimate=pl.CostEstimate(
            flops=8_000_000_000, bytes_accessed=12_000_000, transcendentals=0
        ),
        compiler_params=pltpu.CompilerParams(vmem_limit_bytes=40 * 2**20),
        name="correlate",
    )(info, lhs, table, *mates)


CHAIN = 4
HALVES = 2
ARRIVAL = (
    ((0, 1), (1, 0), (1, 1), (2, 0), (3, 0), (2, 1), (3, 1)),
    ((1, 1), (0, 0), (2, 0), (0, 1), (3, 0), (2, 1), (3, 1)),
    ((2, 1), (3, 0), (1, 0), (3, 1), (0, 0), (1, 1), (0, 1)),
    ((3, 1), (2, 0), (2, 1), (1, 0), (0, 0), (1, 1), (0, 1)),
)
STEPS = 8
TURN_AFTER = {4: (0,), 6: (1, 2), 7: (3,)}


def plan_links():
    last = CHAIN - 1
    queue = {}
    for c in range(CHAIN):
        down = [(b, 0, h) for b in range(c, CHAIN) for h in range(HALVES)] + [(last, 1, 1)]
        up = [(b, 0, h) for b in range(c, -1, -1) for h in range(HALVES)] + [(0, 1, 1)]
        if c > 0:
            queue[c, "down"] = down
        if c < last:
            queue[c, "up"] = up
        near = [b for b in (range(c + 1, CHAIN) if c == 0 else range(c - 1, -1, -1))]
        if c == 1:
            near = [0, 2, 3]
        if c == 2:
            near = [3, 1, 0]
        swap = [(c, 0, 0), (c, 0, 1)]
        for b in near:
            by_chain = (b == last and c < last) or (b == 0 and c > 0)
            swap += [(b, 0, h) for h in range(HALVES) if not (by_chain and h == 1)]
        queue[c, "swap"] = swap
    have = {(c, (c, 0, h)): 0 for c in range(CHAIN) for h in range(HALVES)}
    start = {key: [] for key in queue}
    for t in range(STEPS):
        new = {}
        for (c, way), items in queue.items():
            at = len(start[c, way])
            if at < len(items) and have.get((c, items[at]), 99) <= t:
                start[c, way].append(t)
                b, sw, h = items[at]
                if way == "swap":
                    new[c, (b, 1 - sw, h)] = t + 1
                else:
                    new[c + (1 if way == "up" else -1), (b, sw, h)] = t + 1
        for key, when in new.items():
            assert key not in have
            have[key] = when
    waits = {(c, t): [] for c in range(CHAIN) for t in range(STEPS)}
    sends = {(c, t): [] for c in range(CHAIN) for t in range(STEPS)}
    for (c, item), when in have.items():
        if when > 0:
            waits[c, when].append(item)
    for (c, way), items in queue.items():
        assert len(start[c, way]) == len(items)
        for item, t in zip(items, start[c, way]):
            sends[c, max(t - 1, have[c, item], 0)].append((way, item))
    for c in range(CHAIN):
        for k in range(ROUNDS):
            step = [t for t, turns in TURN_AFTER.items() if k in turns][0]
            for b, sw in ARRIVAL[c][k : k + 4]:
                for h in range(HALVES):
                    assert have[c, (b, sw, h)] <= step
    return waits, sends


def fused_kernel(
    pick_ref, spec_ref, order_ref, table_ref, out_ref,
    blocks, lhs, cross, keep, give, beside, passed, across,
    swap_sem, chain_sem, got_sem, give_sem, beside_sem, passed_sem, across_sem,
):
    nf, _, nw, nc = spec_ref.shape
    part = nf // HALVES
    share = nc // 4
    lag_rows = share * LAGS
    pair = lax.axis_index("pair")
    win = lax.axis_index("win")
    c, x = pair // 2, pair % 2
    row, core = win // 2, win % 2
    swap_to = {"pair": pair + 1 - 2 * x}
    core_to = {"win": win + 1 - 2 * core}
    row_to = {"win": win + 2 - 4 * row}
    waits, sends = plan_links()

    def signal(to):
        pl.semaphore_signal(
            pltpu.get_barrier_semaphore(), inc=1, device_id=to,
            device_id_type=pl.DeviceIdType.MESH,
        )

    signal(swap_to)
    signal(core_to)
    signal(row_to)

    @pl.when(c > 0)
    def _():
        signal({"pair": pair - 2})

    @pl.when(c < CHAIN - 1)
    def _():
        signal({"pair": pair + 2})

    @pl.when((c > 0) & (c < CHAIN - 1))
    def _():
        pl.semaphore_wait(pltpu.get_barrier_semaphore(), 5)

    @pl.when((c == 0) | (c == CHAIN - 1))
    def _():
        pl.semaphore_wait(pltpu.get_barrier_semaphore(), 4)

    def copy(way, item):
        b, sw, h = item
        q = 2 * b + (x if sw == 0 else 1 - x)
        ref = blocks.at[q, pl.ds(h * part, part)]
        if way == "swap":
            sem, to = swap_sem.at[b, h], swap_to
        else:
            side = 0 if way == "down" else 1
            sem = chain_sem.at[side, 2 * b + sw, h]
            to = {"pair": pair - 2 if way == "down" else pair + 2}
        return pltpu.make_async_remote_copy(
            src_ref=ref, dst_ref=ref, send_sem=sem, recv_sem=got_sem.at[q, h],
            device_id=to, device_id_type=pl.DeviceIdType.MESH,
        )

    def links(t, only=None):
        for cs in range(CHAIN):

            @pl.when(c == cs)
            def _(cs=cs):
                if only in (None, 0):
                    for item in waits[cs, t]:
                        copy("swap", item).wait_recv()
                for way, item in sends[cs, t]:
                    if only is None or item[2] == only:
                        copy(way, item).start()

    def square(f, carry):
        re = spec_ref[f, 0].astype(F32)
        im = spec_ref[f, 1].astype(F32)
        out_ref[pl.ds(pl.multiple_of((f + 2) * nw, 8), nw)] = re * re + im * im
        return carry

    zero = jnp.zeros((nw, nc), F32)
    for edge in (0, 1, nf + 2, nf + 3):
        out_ref[pl.ds(edge * nw, nw)] = zero
    lax.fori_loop(0, nf, square, 0)
    rows = lax.broadcasted_iota(jnp.int32, (nc, nc), 0)
    cols = lax.broadcasted_iota(jnp.int32, (nc, nc), 1)

    def scale(f, carry):
        pick = (rows == order_ref[...]).astype(F32).astype(BF)
        total = out_ref[pl.ds(pl.multiple_of(f * nw, 8), nw)]
        for d in range(1, 5):
            total += out_ref[pl.ds(pl.multiple_of((f + d) * nw, 8), nw)]
        count = jnp.minimum(f + 2, nf - 1) - jnp.maximum(f - 2, 0) + 1
        mean = total / count.astype(F32)
        inv = 1.0 / jnp.maximum(jnp.sqrt(mean), 0.5)
        white = jnp.concatenate(
            [
                (spec_ref[f, 0].astype(F32) * inv).astype(BF),
                (spec_ref[f, 1].astype(F32) * inv).astype(BF),
            ],
            0,
        )
        blocks[pair, f] = jnp.dot(white, pick, preferred_element_type=F32).astype(BF)
        return carry

    for h in range(HALVES):
        lax.fori_loop(h * part, (h + 1) * part, scale, 0)
        links(0, h)

    def turn_bin(f, carry):
        eye = (rows == cols).astype(F32).astype(BF)
        turned = lax.dot_general(
            eye, blocks[pair, f], (((1,), (1,)), ((), ())), preferred_element_type=F32
        )
        lhs[f] = turned.astype(BF)
        return carry

    lax.fori_loop(0, nf, turn_bin, 0)

    def to_core(k):
        return pltpu.make_async_remote_copy(
            src_ref=give.at[k % 2], dst_ref=beside.at[k], send_sem=give_sem.at[k],
            recv_sem=beside_sem.at[k], device_id=core_to,
            device_id_type=pl.DeviceIdType.MESH,
        )

    def to_row(k):
        return pltpu.make_async_remote_copy(
            src_ref=passed.at[k], dst_ref=across.at[k], send_sem=passed_sem.at[k],
            recv_sem=across_sem.at[k], device_id=row_to,
            device_id_type=pl.DeviceIdType.MESH,
        )

    def correlate_turn(k):
        places = []
        for m in range(4):
            at = jnp.int32(0)
            for cs in range(CHAIN):
                b, sw = ARRIVAL[cs][k + m]
                at = at + (c == cs).astype(jnp.int32) * (2 * b + (x if sw == 0 else 1 - x))
            places.append(at)

        def one_bin(f, carry):
            right = None
            for m in range(4):
                weight = (pick_ref[k] == m).astype(F32)
                term = blocks[places[m], f] * jnp.full((1, nc), weight, F32).astype(BF)
                right = term if right is None else right + term
            turned = jnp.concatenate([right[nw:], -right[:nw]], 0)
            left = lhs[f]
            cross[f] = jnp.dot(left, right, preferred_element_type=F32).astype(BF)
            cross[nf + f] = jnp.dot(left, turned, preferred_element_type=F32).astype(BF)
            return carry

        lax.fori_loop(0, nf, one_bin, 0)
        if k >= 2:
            to_core(k - 2).wait_send()

        def lags_of(half, other, u):
            owner = lax.rem(row + half, 2) * 2 + lax.rem(core + other, 2)
            start = pl.multiple_of(owner * share + u * GROUP, GROUP)
            right = cross[:, pl.ds(start, GROUP), :].reshape(2 * nf * GROUP, nc)
            return jnp.dot(table_ref[...], right, preferred_element_type=F32)

        size = GROUP * LAGS

        def send_group(u, carry):
            for half in range(2):
                at = pl.multiple_of(half * lag_rows + u * size, size)
                give[k % 2, pl.ds(at, size)] = lags_of(half, 1, u).astype(BF)
            return carry

        def keep_group(u, carry):
            at = pl.multiple_of(u * size, size)
            keep[pl.ds(at, size)] = lags_of(1, 0, u)
            to = pl.multiple_of(k * lag_rows + u * size, size)
            out_ref[pl.ds(to, size)] = lags_of(0, 0, u)
            return carry

        lax.fori_loop(0, share // GROUP, send_group, 0)
        to_core(k).start()
        lax.fori_loop(0, share // GROUP, keep_group, 0)
        to_core(k).wait_recv()
        passed[k] = (keep[...] + beside[k, pl.ds(lag_rows, lag_rows)].astype(F32)).astype(BF)
        to_row(k).start()
        out_ref[pl.ds(k * lag_rows, lag_rows)] += beside[k, pl.ds(0, lag_rows)].astype(F32)

    for t in range(1, STEPS):
        links(t)
        for k in TURN_AFTER.get(t, ()):
            correlate_turn(k)
    for k in range(ROUNDS):
        to_row(k).wait_recv()
        out_ref[pl.ds(k * lag_rows, lag_rows)] += across[k].astype(F32)
    for k in range(ROUNDS):
        if k >= 2:
            to_core(k).wait_send()
        to_row(k).wait_send()
    for cs in range(CHAIN):

        @pl.when(c == cs)
        def _(cs=cs):
            for t in range(STEPS):
                for way, item in sends[cs, t]:
                    copy(way, item).wait_send()


def fused(pick, spectra, order, table):
    nf, _, nw, nc = spectra.shape
    blocks = lax.axis_size("pair")
    rows = nc // 4 * LAGS
    vmem = pl.BlockSpec(memory_space=pltpu.VMEM)
    dma = pltpu.SemaphoreType.DMA
    return pl.pallas_call(
        fused_kernel,
        out_shape=jax.ShapeDtypeStruct((ROUNDS * rows, nc), F32),
        in_specs=[pl.BlockSpec(memory_space=pltpu.SMEM), vmem, vmem, vmem],
        out_specs=vmem,
        scratch_shapes=[
            pltpu.VMEM((blocks, nf, 2 * nw, nc), BF),
            pltpu.VMEM((nf, nc, 2 * nw), BF),
            pltpu.VMEM((2 * nf, nc, nc), BF),
            pltpu.VMEM((rows, nc), F32),
            pltpu.VMEM((2, 2 * rows, nc), BF),
            pltpu.VMEM((ROUNDS, 2 * rows, nc), BF),
            pltpu.VMEM((ROUNDS, rows, nc), BF),
            pltpu.VMEM((ROUNDS, rows, nc), BF),
            dma((CHAIN, HALVES)),
            dma((2, 2 * CHAIN, HALVES)),
            dma((blocks, HALVES)),
            dma((ROUNDS,)),
            dma((ROUNDS,)),
            dma((ROUNDS,)),
            dma((ROUNDS,)),
        ],
        cost_estimate=pl.CostEstimate(
            flops=16_000_000_000, bytes_accessed=16_000_000, transcendentals=0
        ),
        compiler_params=pltpu.CompilerParams(
            vmem_limit_bytes=60 * 2**20, collective_id=0, has_side_effects=True
        ),
        name="fused",
    )(pick, spectra, order, table)


def local(spectra, channel_order, partners):
    num_blocks = lax.axis_size("pair")
    win_count = lax.axis_size("win")
    nf, _, nw, nc = spectra.shape
    table = make_table(nf, LAGS, nw * win_count)
    spread = (
        table.T[None, :, :, None] * jnp.eye(GROUP, dtype=F32)[:, None, None, :]
    ).reshape(GROUP * LAGS, 2 * nf * GROUP).astype(BF)
    me = lax.axis_index("pair")
    win = lax.axis_index("win")
    if num_blocks == 2 * CHAIN and win_count == 4:
        mine = partners[:, me]
        rank = jnp.zeros_like(mine)
        for c in range(CHAIN):
            for index, (b, sw) in enumerate(ARRIVAL[c]):
                same = (mine // 2 == b) & ((mine % 2 != me % 2) == (sw == 1))
                rank = jnp.where((me // 2 == c) & same, index, rank)
        place = jnp.sum((rank[None, :] < rank[:, None]).astype(jnp.int32), 1)
        turns = jnp.arange(ROUNDS, dtype=jnp.int32)
        pick = jnp.sum(jnp.where(place[None, :] == turns[:, None], rank[None, :], 0), 1) - turns
        sums = fused(pick.astype(jnp.int32), spectra, channel_order, spread)
        sums = sums.reshape(ROUNDS, nc // 4, LAGS, nc)
        ordered = []
        for turn in range(ROUNDS):
            value = sums[ROUNDS - 1]
            for k in range(ROUNDS - 1):
                value = jnp.where(place[turn] == k, sums[k], value)
            ordered.append(value)
        return jnp.stack(ordered, 1)[None]
    own, lhs = whiten(spectra, channel_order)
    row, core = win // 2, win % 2
    results = []
    turned = lax.all_to_all(
        own.reshape(num_blocks, -1), "pair", split_axis=0, concat_axis=0, tiled=True
    )
    for turn in range(ROUNDS):
        arranged = jnp.take(turned, partners[turn], axis=0)
        received = lax.all_to_all(arranged, "pair", split_axis=0, concat_axis=0, tiled=True)
        info = jnp.stack([jnp.int32(0), core, row]).astype(jnp.int32)
        keep, give = correlate(info, lhs, spread, [received.reshape(own.shape)])
        beside = lax.ppermute(give, "win", [(w, w ^ 1) for w in range(win_count)])
        passed = (keep[1] + beside[1].astype(F32)).astype(BF)
        across = lax.ppermute(passed, "win", [(w, w ^ 2) for w in range(win_count)])
        results.append(keep[0] + beside[0].astype(F32) + across.astype(F32))
    return jnp.stack(results, 1)[None]


def solution(mesh):
    return jax.shard_map(
        local,
        mesh=mesh,
        in_specs=(P(None, None, "win", "pair"), P("pair", None), P()),
        out_specs=P("pair", "win", None, None, None),
        check_vma=False,
    )
```

```python
import math

import jax
import jax.numpy as jnp
import ml_dtypes
import numpy as np
from jax import lax
from jax.experimental import pallas as pl
from jax.experimental.pallas import tpu as pltpu
from jax.sharding import PartitionSpec as P

LAGS = 16
ROUNDS = 4
GROUP = 16
BF = jnp.bfloat16
F32 = jnp.float32


def make_table(num_bins, num_lags, window_total):
    bin_freq = np.arange(num_bins, dtype=np.float64)[:, None]
    lag_index = (np.arange(num_lags) - num_lags // 2).astype(np.float64)[None, :]
    phase_angle = math.pi * bin_freq * lag_index / num_bins
    norm_factor = 1.0 / math.sqrt(window_total * num_bins)
    table = np.concatenate([np.cos(phase_angle), -np.sin(phase_angle)], 0) * norm_factor
    spread = table.T[None, :, :, None] * np.eye(GROUP)[:, None, None, :]
    return spread.reshape(GROUP * num_lags, 2 * num_bins * GROUP).astype(ml_dtypes.bfloat16)


def whiten_kernel(spec_ref, order_ref, own_ref, lhs_ref, power):
    nf, _, nw, nc = spec_ref.shape
    zero = jnp.zeros((nw, nc), F32)
    for edge in (0, 1, nf + 2, nf + 3):
        power[edge] = zero

    def square(f, carry):
        re = spec_ref[f, 0].astype(F32)
        im = spec_ref[f, 1].astype(F32)
        power[f + 2] = re * re + im * im
        return carry

    lax.fori_loop(0, nf, square, 0)
    rows = lax.broadcasted_iota(jnp.int32, (nc, nc), 0)
    cols = lax.broadcasted_iota(jnp.int32, (nc, nc), 1)
    pick = (rows == order_ref[...]).astype(F32).astype(BF)
    eye = (rows == cols).astype(F32).astype(BF)

    def scale(f, carry):
        total = power[f] + power[f + 1] + power[f + 2] + power[f + 3] + power[f + 4]
        count = jnp.minimum(f + 2, nf - 1) - jnp.maximum(f - 2, 0) + 1
        mean = total / count.astype(F32)
        inv = 1.0 / jnp.maximum(jnp.sqrt(mean), 0.5)
        white = jnp.concatenate(
            [
                (spec_ref[f, 0].astype(F32) * inv).astype(BF),
                (spec_ref[f, 1].astype(F32) * inv).astype(BF),
            ],
            0,
        )
        own = jnp.dot(white, pick, preferred_element_type=F32).astype(BF)
        own_ref[f] = own
        turned = lax.dot_general(eye, own, (((1,), (1,)), ((), ())), preferred_element_type=F32)
        lhs_ref[f] = turned.astype(BF)
        return carry

    lax.fori_loop(0, nf, scale, 0)


def whiten(spectra, order):
    nf, _, nw, nc = spectra.shape
    vmem = pl.BlockSpec(memory_space=pltpu.VMEM)
    return pl.pallas_call(
        whiten_kernel,
        out_shape=(
            jax.ShapeDtypeStruct((nf, 2 * nw, nc), BF),
            jax.ShapeDtypeStruct((nf, nc, 2 * nw), BF),
        ),
        in_specs=[vmem, vmem],
        out_specs=(vmem, vmem),
        scratch_shapes=[pltpu.VMEM((nf + 4, nw, nc), F32)],
        compiler_params=pltpu.CompilerParams(vmem_limit_bytes=40 * 2**20),
        name="whiten",
    )(spectra, order)


def corr_kernel(info_ref, lhs_ref, table_ref, *refs):
    mates = refs[:-5]
    keep_ref, send_ref, mate, cross, sem = refs[-5:]
    nf, nk, nc = mate.shape
    nw = nk // 2
    slot, core, row = info_ref[0], info_ref[1], info_ref[2]
    for s, ref in enumerate(mates):

        @pl.when(slot == s)
        def _(ref=ref):
            pltpu.make_async_copy(ref, mate, sem).start()

    pltpu.make_async_copy(mates[0], mate, sem).wait()

    def one_bin(f, carry):
        right = mate[f]
        turned = jnp.concatenate([right[nw:], -right[:nw]], 0)
        left = lhs_ref[f]
        cross[f] = jnp.dot(left, right, preferred_element_type=F32).astype(BF)
        cross[nf + f] = jnp.dot(left, turned, preferred_element_type=F32).astype(BF)
        return carry

    lax.fori_loop(0, nf, one_bin, 0)
    share = keep_ref.shape[1]
    per = share // GROUP

    def one_group(step, carry):
        half, u = step // per, step % per
        for other, out_ref in ((0, keep_ref), (1, send_ref)):
            owner = lax.rem(row + half, 2) * 2 + lax.rem(core + other, 2)
            start = pl.multiple_of(owner * share + u * GROUP, GROUP)
            right = cross[:, pl.ds(start, GROUP), :].reshape(2 * nf * GROUP, nc)
            lags = jnp.dot(table_ref[...], right, preferred_element_type=F32)
            at = pl.multiple_of(u * GROUP, GROUP)
            out_ref[half, pl.ds(at, GROUP)] = lags.reshape(GROUP, LAGS, nc).astype(out_ref.dtype)
        return carry

    lax.fori_loop(0, 2 * per, one_group, 0)


def correlate(info, lhs, table, mates):
    nf, nc, nk = lhs.shape
    vmem = pl.BlockSpec(memory_space=pltpu.VMEM)
    return pl.pallas_call(
        corr_kernel,
        out_shape=(
            jax.ShapeDtypeStruct((2, nc // 4, LAGS, nc), F32),
            jax.ShapeDtypeStruct((2, nc // 4, LAGS, nc), BF),
        ),
        in_specs=[pl.BlockSpec(memory_space=pltpu.SMEM), vmem, vmem]
        + [pl.BlockSpec(memory_space=pl.ANY)] * len(mates),
        out_specs=(vmem, vmem),
        scratch_shapes=[
            pltpu.VMEM((nf, nk, nc), BF),
            pltpu.VMEM((2 * nf, nc, nc), BF),
            pltpu.SemaphoreType.DMA,
        ],
        cost_estimate=pl.CostEstimate(
            flops=8_000_000_000, bytes_accessed=12_000_000, transcendentals=0
        ),
        compiler_params=pltpu.CompilerParams(vmem_limit_bytes=40 * 2**20),
        name="correlate",
    )(info, lhs, table, *mates)


CHAIN = 4
HALVES = 2
ARRIVAL = (
    ((0, 1), (1, 0), (1, 1), (2, 0), (3, 0), (2, 1), (3, 1)),
    ((1, 1), (0, 0), (2, 0), (0, 1), (3, 0), (2, 1), (3, 1)),
    ((2, 1), (3, 0), (1, 0), (3, 1), (0, 0), (1, 1), (0, 1)),
    ((3, 1), (2, 0), (2, 1), (1, 0), (0, 0), (1, 1), (0, 1)),
)
STEPS = 8
TURN_AFTER = {4: (0,), 6: (1, 2), 7: (3,)}


def plan_links():
    last = CHAIN - 1
    queue = {}
    for c in range(CHAIN):
        down = [(b, 0, h) for b in range(c, CHAIN) for h in range(HALVES)] + [(last, 1, 1)]
        up = [(b, 0, h) for b in range(c, -1, -1) for h in range(HALVES)] + [(0, 1, 1)]
        if c > 0:
            queue[c, "down"] = down
        if c < last:
            queue[c, "up"] = up
        near = [b for b in (range(c + 1, CHAIN) if c == 0 else range(c - 1, -1, -1))]
        if c == 1:
            near = [0, 2, 3]
        if c == 2:
            near = [3, 1, 0]
        swap = [(c, 0, 0), (c, 0, 1)]
        for b in near:
            by_chain = (b == last and c < last) or (b == 0 and c > 0)
            swap += [(b, 0, h) for h in range(HALVES) if not (by_chain and h == 1)]
        queue[c, "swap"] = swap
    have = {(c, (c, 0, h)): 0 for c in range(CHAIN) for h in range(HALVES)}
    start = {key: [] for key in queue}
    for t in range(STEPS):
        new = {}
        for (c, way), items in queue.items():
            at = len(start[c, way])
            if at < len(items) and have.get((c, items[at]), 99) <= t:
                start[c, way].append(t)
                b, sw, h = items[at]
                if way == "swap":
                    new[c, (b, 1 - sw, h)] = t + 1
                else:
                    new[c + (1 if way == "up" else -1), (b, sw, h)] = t + 1
        for key, when in new.items():
            assert key not in have
            have[key] = when
    waits = {(c, t): [] for c in range(CHAIN) for t in range(STEPS)}
    sends = {(c, t): [] for c in range(CHAIN) for t in range(STEPS)}
    for (c, item), when in have.items():
        if when > 0:
            waits[c, when].append(item)
    for (c, way), items in queue.items():
        assert len(start[c, way]) == len(items)
        for item, t in zip(items, start[c, way]):
            sends[c, max(t - 1, have[c, item], 0)].append((way, item))
    for c in range(CHAIN):
        for k in range(ROUNDS):
            step = [t for t, turns in TURN_AFTER.items() if k in turns][0]
            for b, sw in ARRIVAL[c][k : k + 4]:
                for h in range(HALVES):
                    assert have[c, (b, sw, h)] <= step
    return waits, sends


def fused_kernel(
    pick_ref, spec_ref, order_ref, table_ref, out_ref,
    blocks, lhs, cross, keep, give, beside, passed, across,
    swap_sem, chain_sem, got_sem, give_sem, beside_sem, passed_sem, across_sem,
):
    nf, _, nw, nc = spec_ref.shape
    part = nf // HALVES
    share = nc // 4
    lag_rows = share * LAGS
    pair = lax.axis_index("pair")
    win = lax.axis_index("win")
    c, x = pair // 2, pair % 2
    row, core = win // 2, win % 2
    swap_to = {"pair": pair + 1 - 2 * x}
    core_to = {"win": win + 1 - 2 * core}
    row_to = {"win": win + 2 - 4 * row}
    waits, sends = plan_links()

    def signal(to):
        pl.semaphore_signal(
            pltpu.get_barrier_semaphore(), inc=1, device_id=to,
            device_id_type=pl.DeviceIdType.MESH,
        )

    signal(swap_to)
    signal(core_to)
    signal(row_to)

    @pl.when(c > 0)
    def _():
        signal({"pair": pair - 2})

    @pl.when(c < CHAIN - 1)
    def _():
        signal({"pair": pair + 2})

    @pl.when((c > 0) & (c < CHAIN - 1))
    def _():
        pl.semaphore_wait(pltpu.get_barrier_semaphore(), 5)

    @pl.when((c == 0) | (c == CHAIN - 1))
    def _():
        pl.semaphore_wait(pltpu.get_barrier_semaphore(), 4)

    def copy(way, item):
        b, sw, h = item
        q = 2 * b + (x if sw == 0 else 1 - x)
        ref = blocks.at[q, pl.ds(h * part, part)]
        if way == "swap":
            sem, to = swap_sem.at[b, h], swap_to
        else:
            side = 0 if way == "down" else 1
            sem = chain_sem.at[side, 2 * b + sw, h]
            to = {"pair": pair - 2 if way == "down" else pair + 2}
        return pltpu.make_async_remote_copy(
            src_ref=ref, dst_ref=ref, send_sem=sem, recv_sem=got_sem.at[q, h],
            device_id=to, device_id_type=pl.DeviceIdType.MESH,
        )

    def links(t, only=None):
        for cs in range(CHAIN):

            @pl.when(c == cs)
            def _(cs=cs):
                if only in (None, 0):
                    for item in waits[cs, t]:
                        copy("swap", item).wait_recv()
                for way, item in sends[cs, t]:
                    if only is None or item[2] == only:
                        copy(way, item).start()

    def square(f, carry):
        re = spec_ref[f, 0].astype(F32)
        im = spec_ref[f, 1].astype(F32)
        out_ref[pl.ds(pl.multiple_of((f + 2) * nw, 8), nw)] = re * re + im * im
        return carry

    zero = jnp.zeros((nw, nc), F32)
    for edge in (0, 1, nf + 2, nf + 3):
        out_ref[pl.ds(edge * nw, nw)] = zero
    lax.fori_loop(0, nf, square, 0)
    rows = lax.broadcasted_iota(jnp.int32, (nc, nc), 0)
    cols = lax.broadcasted_iota(jnp.int32, (nc, nc), 1)

    def scale(f, carry):
        pick = (rows == order_ref[...]).astype(F32).astype(BF)
        total = out_ref[pl.ds(pl.multiple_of(f * nw, 8), nw)]
        for d in range(1, 5):
            total += out_ref[pl.ds(pl.multiple_of((f + d) * nw, 8), nw)]
        count = jnp.minimum(f + 2, nf - 1) - jnp.maximum(f - 2, 0) + 1
        mean = total / count.astype(F32)
        inv = 1.0 / jnp.maximum(jnp.sqrt(mean), 0.5)
        white = jnp.concatenate(
            [
                (spec_ref[f, 0].astype(F32) * inv).astype(BF),
                (spec_ref[f, 1].astype(F32) * inv).astype(BF),
            ],
            0,
        )
        blocks[pair, f] = jnp.dot(white, pick, preferred_element_type=F32).astype(BF)
        return carry

    for h in range(HALVES):
        lax.fori_loop(h * part, (h + 1) * part, scale, 0, unroll=2)
        links(0, h)

    def turn_bin(f, carry):
        eye = (rows == cols).astype(F32).astype(BF)
        turned = lax.dot_general(
            eye, blocks[pair, f], (((1,), (1,)), ((), ())), preferred_element_type=F32
        )
        lhs[f] = turned.astype(BF)
        return carry

    lax.fori_loop(0, nf, turn_bin, 0, unroll=4)

    def to_core(k):
        return pltpu.make_async_remote_copy(
            src_ref=give.at[k % 2], dst_ref=beside.at[k], send_sem=give_sem.at[k],
            recv_sem=beside_sem.at[k], device_id=core_to,
            device_id_type=pl.DeviceIdType.MESH,
        )

    def to_row(k):
        return pltpu.make_async_remote_copy(
            src_ref=passed.at[k], dst_ref=across.at[k], send_sem=passed_sem.at[k],
            recv_sem=across_sem.at[k], device_id=row_to,
            device_id_type=pl.DeviceIdType.MESH,
        )

    def correlate_turn(k):
        places = []
        for m in range(4):
            at = jnp.int32(0)
            for cs in range(CHAIN):
                b, sw = ARRIVAL[cs][k + m]
                at = at + (c == cs).astype(jnp.int32) * (2 * b + (x if sw == 0 else 1 - x))
            places.append(at)

        def one_bin(f, carry):
            right = None
            for m in range(4):
                weight = (pick_ref[k] == m).astype(F32)
                term = blocks[places[m], f] * jnp.full((1, nc), weight, F32).astype(BF)
                right = term if right is None else right + term
            turned = jnp.concatenate([right[nw:], -right[:nw]], 0)
            left = lhs[f]
            cross[f] = jnp.dot(left, right, preferred_element_type=F32).astype(BF)
            cross[nf + f] = jnp.dot(left, turned, preferred_element_type=F32).astype(BF)
            return carry

        lax.fori_loop(0, nf, one_bin, 0, unroll=4)
        if k >= 2:
            to_core(k - 2).wait_send()

        def lags_of(half, other, u):
            owner = lax.rem(row + half, 2) * 2 + lax.rem(core + other, 2)
            start = pl.multiple_of(owner * share + u * GROUP, GROUP)
            right = cross[:, pl.ds(start, GROUP), :].reshape(2 * nf * GROUP, nc)
            return jnp.dot(table_ref[...], right, preferred_element_type=F32)

        size = GROUP * LAGS

        def send_group(u, carry):
            for half in range(2):
                at = pl.multiple_of(half * lag_rows + u * size, size)
                give[k % 2, pl.ds(at, size)] = lags_of(half, 1, u).astype(BF)
            return carry

        def keep_group(u, carry):
            at = pl.multiple_of(u * size, size)
            keep[pl.ds(at, size)] = lags_of(1, 0, u)
            to = pl.multiple_of(k * lag_rows + u * size, size)
            out_ref[pl.ds(to, size)] = lags_of(0, 0, u)
            return carry

        lax.fori_loop(0, share // GROUP, send_group, 0, unroll=2)
        to_core(k).start()
        lax.fori_loop(0, share // GROUP, keep_group, 0, unroll=2)
        to_core(k).wait_recv()
        passed[k] = (keep[...] + beside[k, pl.ds(lag_rows, lag_rows)].astype(F32)).astype(BF)
        to_row(k).start()
        out_ref[pl.ds(k * lag_rows, lag_rows)] += beside[k, pl.ds(0, lag_rows)].astype(F32)

    for t in range(1, STEPS):
        links(t)
        for k in TURN_AFTER.get(t, ()):
            correlate_turn(k)
    for k in range(ROUNDS):
        to_row(k).wait_recv()
        out_ref[pl.ds(k * lag_rows, lag_rows)] += across[k].astype(F32)
    for k in range(ROUNDS):
        if k >= 2:
            to_core(k).wait_send()
        to_row(k).wait_send()
    for cs in range(CHAIN):

        @pl.when(c == cs)
        def _(cs=cs):
            for t in range(STEPS):
                for way, item in sends[cs, t]:
                    copy(way, item).wait_send()


def fused(pick, spectra, order, table):
    nf, _, nw, nc = spectra.shape
    blocks = lax.axis_size("pair")
    rows = nc // 4 * LAGS
    vmem = pl.BlockSpec(memory_space=pltpu.VMEM)
    dma = pltpu.SemaphoreType.DMA
    return pl.pallas_call(
        fused_kernel,
        out_shape=jax.ShapeDtypeStruct((ROUNDS * rows, nc), F32),
        in_specs=[pl.BlockSpec(memory_space=pltpu.SMEM), vmem, vmem, vmem],
        out_specs=vmem,
        scratch_shapes=[
            pltpu.VMEM((blocks, nf, 2 * nw, nc), BF),
            pltpu.VMEM((nf, nc, 2 * nw), BF),
            pltpu.VMEM((2 * nf, nc, nc), BF),
            pltpu.VMEM((rows, nc), F32),
            pltpu.VMEM((2, 2 * rows, nc), BF),
            pltpu.VMEM((ROUNDS, 2 * rows, nc), BF),
            pltpu.VMEM((ROUNDS, rows, nc), BF),
            pltpu.VMEM((ROUNDS, rows, nc), BF),
            dma((CHAIN, HALVES)),
            dma((2, 2 * CHAIN, HALVES)),
            dma((blocks, HALVES)),
            dma((ROUNDS,)),
            dma((ROUNDS,)),
            dma((ROUNDS,)),
            dma((ROUNDS,)),
        ],
        cost_estimate=pl.CostEstimate(
            flops=16_000_000_000, bytes_accessed=16_000_000, transcendentals=0
        ),
        compiler_params=pltpu.CompilerParams(
            vmem_limit_bytes=60 * 2**20, collective_id=0, has_side_effects=True
        ),
        name="fused",
    )(pick, spectra, order, table)


def arrange_kernel(place_ref, sums_ref, out_ref):
    out_ref[:, 0] = sums_ref[0]


def arrange(place, sums):
    rounds, rows, lags, nc = sums.shape
    part = rows // 2
    return pl.pallas_call(
        arrange_kernel,
        grid_spec=pltpu.PrefetchScalarGridSpec(
            num_scalar_prefetch=1,
            grid=(rounds, 2),
            in_specs=[
                pl.BlockSpec((1, part, lags, nc), lambda r, h, place: (place[r], h, 0, 0))
            ],
            out_specs=pl.BlockSpec((part, 1, lags, nc), lambda r, h, place: (h, r, 0, 0)),
        ),
        out_shape=jax.ShapeDtypeStruct((rows, rounds, lags, nc), F32),
        name="arrange",
    )(place, sums)


def local(spectra, channel_order, partners):
    num_blocks = lax.axis_size("pair")
    win_count = lax.axis_size("win")
    nf, _, nw, nc = spectra.shape
    spread = jnp.asarray(make_table(nf, LAGS, nw * win_count))
    me = lax.axis_index("pair")
    win = lax.axis_index("win")
    if num_blocks == 2 * CHAIN and win_count == 4:
        mine = partners[:, me]
        rank = jnp.zeros_like(mine)
        for c in range(CHAIN):
            for index, (b, sw) in enumerate(ARRIVAL[c]):
                same = (mine // 2 == b) & ((mine % 2 != me % 2) == (sw == 1))
                rank = jnp.where((me // 2 == c) & same, index, rank)
        place = jnp.sum((rank[None, :] < rank[:, None]).astype(jnp.int32), 1)
        turns = jnp.arange(ROUNDS, dtype=jnp.int32)
        pick = jnp.sum(jnp.where(place[None, :] == turns[:, None], rank[None, :], 0), 1) - turns
        sums = fused(pick.astype(jnp.int32), spectra, channel_order, spread)
        return arrange(place, sums.reshape(ROUNDS, nc // 4, LAGS, nc))[None]
    own, lhs = whiten(spectra, channel_order)
    row, core = win // 2, win % 2
    results = []
    turned = lax.all_to_all(
        own.reshape(num_blocks, -1), "pair", split_axis=0, concat_axis=0, tiled=True
    )
    for turn in range(ROUNDS):
        arranged = jnp.take(turned, partners[turn], axis=0)
        received = lax.all_to_all(arranged, "pair", split_axis=0, concat_axis=0, tiled=True)
        info = jnp.stack([jnp.int32(0), core, row]).astype(jnp.int32)
        keep, give = correlate(info, lhs, spread, [received.reshape(own.shape)])
        beside = lax.ppermute(give, "win", [(w, w ^ 1) for w in range(win_count)])
        passed = (keep[1] + beside[1].astype(F32)).astype(BF)
        across = lax.ppermute(passed, "win", [(w, w ^ 2) for w in range(win_count)])
        results.append(keep[0] + beside[0].astype(F32) + across.astype(F32))
    return jnp.stack(results, 1)[None]


def solution(mesh):
    return jax.shard_map(
        local,
        mesh=mesh,
        in_specs=(P(None, None, "win", "pair"), P("pair", None), P()),
        out_specs=P("pair", "win", None, None, None),
        check_vma=False,
    )
```

```python
import functools
import math

import jax
import jax.numpy as jnp
import ml_dtypes
import numpy as np
from jax import lax
from jax.experimental import pallas as pl
from jax.experimental.pallas import tpu as pltpu
from jax.sharding import PartitionSpec as P

LAGS = 16
ROUNDS = 4
GROUP = 16
BF = jnp.bfloat16
F32 = jnp.float32


def make_table(num_bins, num_lags, window_total):
    bin_freq = np.arange(num_bins, dtype=np.float64)[:, None]
    lag_index = (np.arange(num_lags) - num_lags // 2).astype(np.float64)[None, :]
    phase_angle = math.pi * bin_freq * lag_index / num_bins
    norm_factor = 1.0 / math.sqrt(window_total * num_bins)
    table = np.concatenate([np.cos(phase_angle), -np.sin(phase_angle)], 0) * norm_factor
    spread = table.T[None, :, :, None] * np.eye(GROUP)[:, None, None, :]
    return spread.reshape(GROUP * num_lags, 2 * num_bins * GROUP).astype(ml_dtypes.bfloat16)


def whiten_kernel(spec_ref, order_ref, own_ref, lhs_ref, power):
    nf, _, nw, nc = spec_ref.shape
    zero = jnp.zeros((nw, nc), F32)
    for edge in (0, 1, nf + 2, nf + 3):
        power[edge] = zero

    def square(f, carry):
        re = spec_ref[f, 0].astype(F32)
        im = spec_ref[f, 1].astype(F32)
        power[f + 2] = re * re + im * im
        return carry

    lax.fori_loop(0, nf, square, 0, unroll=4)
    rows = lax.broadcasted_iota(jnp.int32, (nc, nc), 0)
    cols = lax.broadcasted_iota(jnp.int32, (nc, nc), 1)
    pick = (rows == order_ref[...]).astype(F32).astype(BF)
    eye = (rows == cols).astype(F32).astype(BF)

    def scale(f, carry):
        total = power[f] + power[f + 1] + power[f + 2] + power[f + 3] + power[f + 4]
        count = jnp.minimum(f + 2, nf - 1) - jnp.maximum(f - 2, 0) + 1
        mean = total / count.astype(F32)
        inv = 1.0 / jnp.maximum(jnp.sqrt(mean), 0.5)
        white = jnp.concatenate(
            [
                (spec_ref[f, 0].astype(F32) * inv).astype(BF),
                (spec_ref[f, 1].astype(F32) * inv).astype(BF),
            ],
            0,
        )
        own = jnp.dot(white, pick, preferred_element_type=F32).astype(BF)
        own_ref[f] = own
        turned = lax.dot_general(eye, own, (((1,), (1,)), ((), ())), preferred_element_type=F32)
        lhs_ref[f] = turned.astype(BF)
        return carry

    lax.fori_loop(0, nf, scale, 0)


def whiten(spectra, order):
    nf, _, nw, nc = spectra.shape
    vmem = pl.BlockSpec(memory_space=pltpu.VMEM)
    return pl.pallas_call(
        whiten_kernel,
        out_shape=(
            jax.ShapeDtypeStruct((nf, 2 * nw, nc), BF),
            jax.ShapeDtypeStruct((nf, nc, 2 * nw), BF),
        ),
        in_specs=[vmem, vmem],
        out_specs=(vmem, vmem),
        scratch_shapes=[pltpu.VMEM((nf + 4, nw, nc), F32)],
        compiler_params=pltpu.CompilerParams(vmem_limit_bytes=40 * 2**20),
        name="whiten",
    )(spectra, order)


def corr_kernel(info_ref, lhs_ref, table_ref, *refs):
    mates = refs[:-5]
    keep_ref, send_ref, mate, cross, sem = refs[-5:]
    nf, nk, nc = mate.shape
    nw = nk // 2
    slot, core, row = info_ref[0], info_ref[1], info_ref[2]
    for s, ref in enumerate(mates):

        @pl.when(slot == s)
        def _(ref=ref):
            pltpu.make_async_copy(ref, mate, sem).start()

    pltpu.make_async_copy(mates[0], mate, sem).wait()

    def one_bin(f, carry):
        right = mate[f]
        turned = jnp.concatenate([right[nw:], -right[:nw]], 0)
        left = lhs_ref[f]
        cross[f] = jnp.dot(left, right, preferred_element_type=F32).astype(BF)
        cross[nf + f] = jnp.dot(left, turned, preferred_element_type=F32).astype(BF)
        return carry

    lax.fori_loop(0, nf, one_bin, 0)
    share = keep_ref.shape[1]
    per = share // GROUP

    def one_group(step, carry):
        half, u = step // per, step % per
        for other, out_ref in ((0, keep_ref), (1, send_ref)):
            owner = lax.rem(row + half, 2) * 2 + lax.rem(core + other, 2)
            start = pl.multiple_of(owner * share + u * GROUP, GROUP)
            right = cross[:, pl.ds(start, GROUP), :].reshape(2 * nf * GROUP, nc)
            lags = jnp.dot(table_ref[...], right, preferred_element_type=F32)
            at = pl.multiple_of(u * GROUP, GROUP)
            out_ref[half, pl.ds(at, GROUP)] = lags.reshape(GROUP, LAGS, nc).astype(out_ref.dtype)
        return carry

    lax.fori_loop(0, 2 * per, one_group, 0)


def correlate(info, lhs, table, mates):
    nf, nc, nk = lhs.shape
    vmem = pl.BlockSpec(memory_space=pltpu.VMEM)
    return pl.pallas_call(
        corr_kernel,
        out_shape=(
            jax.ShapeDtypeStruct((2, nc // 4, LAGS, nc), F32),
            jax.ShapeDtypeStruct((2, nc // 4, LAGS, nc), BF),
        ),
        in_specs=[pl.BlockSpec(memory_space=pltpu.SMEM), vmem, vmem]
        + [pl.BlockSpec(memory_space=pl.ANY)] * len(mates),
        out_specs=(vmem, vmem),
        scratch_shapes=[
            pltpu.VMEM((nf, nk, nc), BF),
            pltpu.VMEM((2 * nf, nc, nc), BF),
            pltpu.SemaphoreType.DMA,
        ],
        cost_estimate=pl.CostEstimate(
            flops=8_000_000_000, bytes_accessed=12_000_000, transcendentals=0
        ),
        compiler_params=pltpu.CompilerParams(vmem_limit_bytes=40 * 2**20),
        name="correlate",
    )(info, lhs, table, *mates)


CHAIN = 4
HALVES = 2
ARRIVAL = (
    ((0, 1), (1, 0), (1, 1), (2, 0), (3, 0), (2, 1), (3, 1)),
    ((1, 1), (0, 0), (2, 0), (0, 1), (3, 0), (2, 1), (3, 1)),
    ((2, 1), (3, 0), (1, 0), (3, 1), (0, 0), (1, 1), (0, 1)),
    ((3, 1), (2, 0), (2, 1), (1, 0), (0, 0), (1, 1), (0, 1)),
)
STEPS = 8
TURN_AFTER = {4: (0,), 6: (1, 2), 7: (3,)}


def plan_links():
    last = CHAIN - 1
    queue = {}
    for c in range(CHAIN):
        down = [(b, 0, h) for b in range(c, CHAIN) for h in range(HALVES)] + [(last, 1, 1)]
        up = [(b, 0, h) for b in range(c, -1, -1) for h in range(HALVES)] + [(0, 1, 1)]
        if c > 0:
            queue[c, "down"] = down
        if c < last:
            queue[c, "up"] = up
        near = [b for b in (range(c + 1, CHAIN) if c == 0 else range(c - 1, -1, -1))]
        if c == 1:
            near = [0, 2, 3]
        if c == 2:
            near = [3, 1, 0]
        swap = [(c, 0, 0), (c, 0, 1)]
        for b in near:
            by_chain = (b == last and c < last) or (b == 0 and c > 0)
            swap += [(b, 0, h) for h in range(HALVES) if not (by_chain and h == 1)]
        queue[c, "swap"] = swap
    have = {(c, (c, 0, h)): 0 for c in range(CHAIN) for h in range(HALVES)}
    start = {key: [] for key in queue}
    for t in range(STEPS):
        new = {}
        for (c, way), items in queue.items():
            at = len(start[c, way])
            if at < len(items) and have.get((c, items[at]), 99) <= t:
                start[c, way].append(t)
                b, sw, h = items[at]
                if way == "swap":
                    new[c, (b, 1 - sw, h)] = t + 1
                else:
                    new[c + (1 if way == "up" else -1), (b, sw, h)] = t + 1
        for key, when in new.items():
            assert key not in have
            have[key] = when
    waits = {(c, t): [] for c in range(CHAIN) for t in range(STEPS)}
    sends = {(c, t): [] for c in range(CHAIN) for t in range(STEPS)}
    for (c, item), when in have.items():
        if when > 0:
            waits[c, when].append(item)
    for (c, way), items in queue.items():
        assert len(start[c, way]) == len(items)
        for item, t in zip(items, start[c, way]):
            sends[c, max(t - 1, have[c, item], 0)].append((way, item))
    for c in range(CHAIN):
        for k in range(ROUNDS):
            step = [t for t, turns in TURN_AFTER.items() if k in turns][0]
            for b, sw in ARRIVAL[c][k : k + 4]:
                for h in range(HALVES):
                    assert have[c, (b, sw, h)] <= step
    return waits, sends


def fused_kernel(
    pick_ref, spec_ref, order_ref, table_ref, out_ref,
    blocks, lhs, cross, perm, keep, give, beside, passed, across,
    swap_sem, chain_sem, got_sem, give_sem, beside_sem, passed_sem, across_sem,
):
    nf, _, nw, nc = spec_ref.shape
    part = nf // HALVES
    share = nc // 4
    lag_rows = share * LAGS
    pair = lax.axis_index("pair")
    win = lax.axis_index("win")
    c, x = pair // 2, pair % 2
    row, core = win // 2, win % 2
    swap_to = {"pair": pair + 1 - 2 * x}
    core_to = {"win": win + 1 - 2 * core}
    row_to = {"win": win + 2 - 4 * row}
    waits, sends = plan_links()

    def signal(to):
        pl.semaphore_signal(
            pltpu.get_barrier_semaphore(), inc=1, device_id=to,
            device_id_type=pl.DeviceIdType.MESH,
        )

    signal(swap_to)
    signal(core_to)
    signal(row_to)

    @pl.when(c > 0)
    def _():
        signal({"pair": pair - 2})

    @pl.when(c < CHAIN - 1)
    def _():
        signal({"pair": pair + 2})

    def greet():
        @pl.when((c > 0) & (c < CHAIN - 1))
        def _():
            pl.semaphore_wait(pltpu.get_barrier_semaphore(), 5)

        @pl.when((c == 0) | (c == CHAIN - 1))
        def _():
            pl.semaphore_wait(pltpu.get_barrier_semaphore(), 4)

    def copy(way, item):
        b, sw, h = item
        q = 2 * b + (x if sw == 0 else 1 - x)
        ref = blocks.at[q, pl.ds(h * part, part)]
        if way == "swap":
            sem, to = swap_sem.at[b, h], swap_to
        else:
            side = 0 if way == "down" else 1
            sem = chain_sem.at[side, 2 * b + sw, h]
            to = {"pair": pair - 2 if way == "down" else pair + 2}
        return pltpu.make_async_remote_copy(
            src_ref=ref, dst_ref=ref, send_sem=sem, recv_sem=got_sem.at[q, h],
            device_id=to, device_id_type=pl.DeviceIdType.MESH,
        )

    def links(t, only=None):
        for cs in range(CHAIN):

            @pl.when(c == cs)
            def _(cs=cs):
                if only in (None, 0):
                    for item in waits[cs, t]:
                        copy("swap", item).wait_recv()
                for way, item in sends[cs, t]:
                    if only is None or item[2] == only:
                        copy(way, item).start()

    def square(f, carry):
        re = spec_ref[f, 0].astype(F32)
        im = spec_ref[f, 1].astype(F32)
        out_ref[pl.ds(pl.multiple_of((f + 2) * nw, 8), nw)] = re * re + im * im
        return carry

    zero = jnp.zeros((nw, nc), F32)
    for edge in (0, 1, nf + 2, nf + 3):
        out_ref[pl.ds(edge * nw, nw)] = zero
    lax.fori_loop(0, nf, square, 0, unroll=4)
    rows = lax.broadcasted_iota(jnp.int32, (nc, nc), 0)
    cols = lax.broadcasted_iota(jnp.int32, (nc, nc), 1)
    perm[0] = (rows == order_ref[...]).astype(F32).astype(BF)
    perm[1] = (rows == cols).astype(F32).astype(BF)

    def scale(f, carry):
        total = out_ref[pl.ds(pl.multiple_of(f * nw, 8), nw)]
        for d in range(1, 5):
            total += out_ref[pl.ds(pl.multiple_of((f + d) * nw, 8), nw)]
        count = jnp.minimum(f + 2, nf - 1) - jnp.maximum(f - 2, 0) + 1
        mean = total / count.astype(F32)
        inv = 1.0 / jnp.maximum(jnp.sqrt(mean), 0.5)
        white = jnp.concatenate(
            [
                (spec_ref[f, 0].astype(F32) * inv).astype(BF),
                (spec_ref[f, 1].astype(F32) * inv).astype(BF),
            ],
            0,
        )
        blocks[pair, f] = jnp.dot(white, perm[0], preferred_element_type=F32).astype(BF)
        return carry

    greet()
    for h in range(HALVES):
        lax.fori_loop(h * part, (h + 1) * part, scale, 0, unroll=4)
        links(0, h)

    def turn_bin(f, carry):
        turned = lax.dot_general(
            perm[1], blocks[pair, f], (((1,), (1,)), ((), ())), preferred_element_type=F32
        )
        lhs[f] = turned.astype(BF)
        return carry

    lax.fori_loop(0, nf, turn_bin, 0, unroll=4)

    def to_core(k, half):
        at = pl.ds(half * lag_rows, lag_rows)
        return pltpu.make_async_remote_copy(
            src_ref=give.at[k % 2, at], dst_ref=beside.at[k, at],
            send_sem=give_sem.at[k, half], recv_sem=beside_sem.at[k, half],
            device_id=core_to, device_id_type=pl.DeviceIdType.MESH,
        )

    def to_row(k):
        return pltpu.make_async_remote_copy(
            src_ref=passed.at[k], dst_ref=across.at[k], send_sem=passed_sem.at[k],
            recv_sem=across_sem.at[k], device_id=row_to,
            device_id_type=pl.DeviceIdType.MESH,
        )

    def correlate_turn(k):
        places = []
        for m in range(4):
            at = jnp.int32(0)
            for cs in range(CHAIN):
                b, sw = ARRIVAL[cs][k + m]
                at = at + (c == cs).astype(jnp.int32) * (2 * b + (x if sw == 0 else 1 - x))
            places.append(at)

        def one_bin(f, carry):
            right = None
            for m in range(4):
                weight = (pick_ref[k] == m).astype(F32)
                term = blocks[places[m], f] * jnp.full((1, nc), weight, F32).astype(BF)
                right = term if right is None else right + term
            turned = jnp.concatenate([right[nw:], -right[:nw]], 0)
            left = lhs[f]
            cross[f] = jnp.dot(left, right, preferred_element_type=F32).astype(BF)
            cross[nf + f] = jnp.dot(left, turned, preferred_element_type=F32).astype(BF)
            return carry

        lax.fori_loop(0, nf, one_bin, 0, unroll=4)
        if k >= 2:
            for half in range(2):
                to_core(k - 2, half).wait_send()

        def lags_of(half, other, u):
            owner = lax.rem(row + half, 2) * 2 + lax.rem(core + other, 2)
            start = pl.multiple_of(owner * share + u * GROUP, GROUP)
            right = cross[:, pl.ds(start, GROUP), :].reshape(2 * nf * GROUP, nc)
            return jnp.dot(table_ref[...], right, preferred_element_type=F32)

        size = GROUP * LAGS

        def send_group(half, u, carry):
            at = pl.multiple_of(half * lag_rows + u * size, size)
            give[k % 2, pl.ds(at, size)] = lags_of(half, 1, u).astype(BF)
            return carry

        def keep_group(half, u, carry):
            if half == 1:
                keep[pl.ds(pl.multiple_of(u * size, size), size)] = lags_of(1, 0, u)
            else:
                to = pl.multiple_of(k * lag_rows + u * size, size)
                out_ref[pl.ds(to, size)] = lags_of(0, 0, u)
            return carry

        groups = share // GROUP
        for half in (1, 0):
            lax.fori_loop(0, groups, functools.partial(send_group, half), 0, unroll=2)
            to_core(k, half).start()
            lax.fori_loop(0, groups, functools.partial(keep_group, half), 0, unroll=2)
            to_core(k, half).wait_recv()
            got = beside[k, pl.ds(half * lag_rows, lag_rows)].astype(F32)
            if half == 1:
                passed[k] = (keep[...] + got).astype(BF)
                to_row(k).start()
            else:
                out_ref[pl.ds(k * lag_rows, lag_rows)] += got

    for t in range(1, STEPS):
        links(t)
        for k in TURN_AFTER.get(t, ()):
            correlate_turn(k)
    for k in range(ROUNDS):
        to_row(k).wait_recv()
        out_ref[pl.ds(k * lag_rows, lag_rows)] += across[k].astype(F32)
    for k in range(ROUNDS):
        if k >= 2:
            for half in range(2):
                to_core(k, half).wait_send()
        to_row(k).wait_send()
    for cs in range(CHAIN):

        @pl.when(c == cs)
        def _(cs=cs):
            for t in range(STEPS):
                for way, item in sends[cs, t]:
                    copy(way, item).wait_send()


def fused(pick, spectra, order, table):
    nf, _, nw, nc = spectra.shape
    blocks = lax.axis_size("pair")
    rows = nc // 4 * LAGS
    vmem = pl.BlockSpec(memory_space=pltpu.VMEM)
    dma = pltpu.SemaphoreType.DMA
    return pl.pallas_call(
        fused_kernel,
        out_shape=jax.ShapeDtypeStruct((ROUNDS * rows, nc), F32),
        in_specs=[pl.BlockSpec(memory_space=pltpu.SMEM), vmem, vmem, vmem],
        out_specs=vmem,
        scratch_shapes=[
            pltpu.VMEM((blocks, nf, 2 * nw, nc), BF),
            pltpu.VMEM((nf, nc, 2 * nw), BF),
            pltpu.VMEM((2 * nf, nc, nc), BF),
            pltpu.VMEM((2, nc, nc), BF),
            pltpu.VMEM((rows, nc), F32),
            pltpu.VMEM((2, 2 * rows, nc), BF),
            pltpu.VMEM((ROUNDS, 2 * rows, nc), BF),
            pltpu.VMEM((ROUNDS, rows, nc), BF),
            pltpu.VMEM((ROUNDS, rows, nc), BF),
            dma((CHAIN, HALVES)),
            dma((2, 2 * CHAIN, HALVES)),
            dma((blocks, HALVES)),
            dma((ROUNDS, 2)),
            dma((ROUNDS, 2)),
            dma((ROUNDS,)),
            dma((ROUNDS,)),
        ],
        cost_estimate=pl.CostEstimate(
            flops=16_000_000_000, bytes_accessed=16_000_000, transcendentals=0
        ),
        compiler_params=pltpu.CompilerParams(
            vmem_limit_bytes=60 * 2**20, collective_id=0, has_side_effects=True
        ),
        name="fused",
    )(pick, spectra, order, table)


def arrange_kernel(place_ref, sums_ref, out_ref, sem):
    rounds = sums_ref.shape[0]
    copies = [
        pltpu.make_async_copy(sums_ref.at[place_ref[r]], out_ref.at[:, r], sem.at[r])
        for r in range(rounds)
    ]
    for copy in copies:
        copy.start()
    for copy in copies:
        copy.wait()


def arrange(place, sums):
    rounds, rows, lags, nc = sums.shape
    return pl.pallas_call(
        arrange_kernel,
        in_specs=[
            pl.BlockSpec(memory_space=pltpu.SMEM),
            pl.BlockSpec(memory_space=pl.ANY),
        ],
        out_specs=pl.BlockSpec(memory_space=pl.ANY),
        out_shape=jax.ShapeDtypeStruct((rows, rounds, lags, nc), F32),
        scratch_shapes=[pltpu.SemaphoreType.DMA((rounds,))],
        name="arrange",
    )(place, sums)


def local(spectra, channel_order, partners):
    num_blocks = lax.axis_size("pair")
    win_count = lax.axis_size("win")
    nf, _, nw, nc = spectra.shape
    spread = jnp.asarray(make_table(nf, LAGS, nw * win_count))
    me = lax.axis_index("pair")
    win = lax.axis_index("win")
    if num_blocks == 2 * CHAIN and win_count == 4:
        mine = partners[:, me]
        rank = jnp.zeros_like(mine)
        for c in range(CHAIN):
            for index, (b, sw) in enumerate(ARRIVAL[c]):
                same = (mine // 2 == b) & ((mine % 2 != me % 2) == (sw == 1))
                rank = jnp.where((me // 2 == c) & same, index, rank)
        place = jnp.sum((rank[None, :] < rank[:, None]).astype(jnp.int32), 1)
        turns = jnp.arange(ROUNDS, dtype=jnp.int32)
        pick = jnp.sum(jnp.where(place[None, :] == turns[:, None], rank[None, :], 0), 1) - turns
        sums = fused(pick.astype(jnp.int32), spectra, channel_order, spread)
        return arrange(place, sums.reshape(ROUNDS, nc // 4, LAGS, nc))[None]
    own, lhs = whiten(spectra, channel_order)
    row, core = win // 2, win % 2
    results = []
    turned = lax.all_to_all(
        own.reshape(num_blocks, -1), "pair", split_axis=0, concat_axis=0, tiled=True
    )
    for turn in range(ROUNDS):
        arranged = jnp.take(turned, partners[turn], axis=0)
        received = lax.all_to_all(arranged, "pair", split_axis=0, concat_axis=0, tiled=True)
        info = jnp.stack([jnp.int32(0), core, row]).astype(jnp.int32)
        keep, give = correlate(info, lhs, spread, [received.reshape(own.shape)])
        beside = lax.ppermute(give, "win", [(w, w ^ 1) for w in range(win_count)])
        passed = (keep[1] + beside[1].astype(F32)).astype(BF)
        across = lax.ppermute(passed, "win", [(w, w ^ 2) for w in range(win_count)])
        results.append(keep[0] + beside[0].astype(F32) + across.astype(F32))
    return jnp.stack(results, 1)[None]


def solution(mesh):
    return jax.shard_map(
        local,
        mesh=mesh,
        in_specs=(P(None, None, "win", "pair"), P("pair", None), P()),
        out_specs=P("pair", "win", None, None, None),
        check_vma=False,
    )
```

```python
import functools
import math

import jax
import jax.numpy as jnp
import ml_dtypes
import numpy as np
from jax import lax
from jax.experimental import pallas as pl
from jax.experimental.pallas import tpu as pltpu
from jax.sharding import PartitionSpec as P

LAGS = 16
ROUNDS = 4
GROUP = 16
BF = jnp.bfloat16
F32 = jnp.float32


def make_table(num_bins, num_lags, window_total):
    bin_freq = np.arange(num_bins, dtype=np.float64)[:, None]
    lag_index = (np.arange(num_lags) - num_lags // 2).astype(np.float64)[None, :]
    phase_angle = math.pi * bin_freq * lag_index / num_bins
    norm_factor = 1.0 / math.sqrt(window_total * num_bins)
    table = np.concatenate([np.cos(phase_angle), -np.sin(phase_angle)], 0) * norm_factor
    spread = table.T[None, :, :, None] * np.eye(GROUP)[:, None, None, :]
    return spread.reshape(GROUP * num_lags, 2 * num_bins * GROUP).astype(ml_dtypes.bfloat16)


def whiten_kernel(spec_ref, order_ref, own_ref, lhs_ref, power):
    nf, _, nw, nc = spec_ref.shape
    zero = jnp.zeros((nw, nc), F32)
    for edge in (0, 1, nf + 2, nf + 3):
        power[edge] = zero

    def square(f, carry):
        re = spec_ref[f, 0].astype(F32)
        im = spec_ref[f, 1].astype(F32)
        power[f + 2] = re * re + im * im
        return carry

    lax.fori_loop(0, nf, square, 0, unroll=4)
    rows = lax.broadcasted_iota(jnp.int32, (nc, nc), 0)
    cols = lax.broadcasted_iota(jnp.int32, (nc, nc), 1)
    pick = (rows == order_ref[...]).astype(F32).astype(BF)
    eye = (rows == cols).astype(F32).astype(BF)

    def scale(f, carry):
        total = power[f] + power[f + 1] + power[f + 2] + power[f + 3] + power[f + 4]
        count = jnp.minimum(f + 2, nf - 1) - jnp.maximum(f - 2, 0) + 1
        mean = total / count.astype(F32)
        inv = 1.0 / jnp.maximum(jnp.sqrt(mean), 0.5)
        white = jnp.concatenate(
            [
                (spec_ref[f, 0].astype(F32) * inv).astype(BF),
                (spec_ref[f, 1].astype(F32) * inv).astype(BF),
            ],
            0,
        )
        own = jnp.dot(white, pick, preferred_element_type=F32).astype(BF)
        own_ref[f] = own
        turned = lax.dot_general(eye, own, (((1,), (1,)), ((), ())), preferred_element_type=F32)
        lhs_ref[f] = turned.astype(BF)
        return carry

    lax.fori_loop(0, nf, scale, 0)


def whiten(spectra, order):
    nf, _, nw, nc = spectra.shape
    vmem = pl.BlockSpec(memory_space=pltpu.VMEM)
    return pl.pallas_call(
        whiten_kernel,
        out_shape=(
            jax.ShapeDtypeStruct((nf, 2 * nw, nc), BF),
            jax.ShapeDtypeStruct((nf, nc, 2 * nw), BF),
        ),
        in_specs=[vmem, vmem],
        out_specs=(vmem, vmem),
        scratch_shapes=[pltpu.VMEM((nf + 4, nw, nc), F32)],
        compiler_params=pltpu.CompilerParams(vmem_limit_bytes=40 * 2**20),
        name="whiten",
    )(spectra, order)


def corr_kernel(info_ref, lhs_ref, table_ref, *refs):
    mates = refs[:-5]
    keep_ref, send_ref, mate, cross, sem = refs[-5:]
    nf, nk, nc = mate.shape
    nw = nk // 2
    slot, core, row = info_ref[0], info_ref[1], info_ref[2]
    for s, ref in enumerate(mates):

        @pl.when(slot == s)
        def _(ref=ref):
            pltpu.make_async_copy(ref, mate, sem).start()

    pltpu.make_async_copy(mates[0], mate, sem).wait()

    def one_bin(f, carry):
        right = mate[f]
        turned = jnp.concatenate([right[nw:], -right[:nw]], 0)
        left = lhs_ref[f]
        cross[f] = jnp.dot(left, right, preferred_element_type=F32).astype(BF)
        cross[nf + f] = jnp.dot(left, turned, preferred_element_type=F32).astype(BF)
        return carry

    lax.fori_loop(0, nf, one_bin, 0)
    share = keep_ref.shape[1]
    per = share // GROUP

    def one_group(step, carry):
        half, u = step // per, step % per
        for other, out_ref in ((0, keep_ref), (1, send_ref)):
            owner = lax.rem(row + half, 2) * 2 + lax.rem(core + other, 2)
            start = pl.multiple_of(owner * share + u * GROUP, GROUP)
            right = cross[:, pl.ds(start, GROUP), :].reshape(2 * nf * GROUP, nc)
            lags = jnp.dot(table_ref[...], right, preferred_element_type=F32)
            at = pl.multiple_of(u * GROUP, GROUP)
            out_ref[half, pl.ds(at, GROUP)] = lags.reshape(GROUP, LAGS, nc).astype(out_ref.dtype)
        return carry

    lax.fori_loop(0, 2 * per, one_group, 0)


def correlate(info, lhs, table, mates):
    nf, nc, nk = lhs.shape
    vmem = pl.BlockSpec(memory_space=pltpu.VMEM)
    return pl.pallas_call(
        corr_kernel,
        out_shape=(
            jax.ShapeDtypeStruct((2, nc // 4, LAGS, nc), F32),
            jax.ShapeDtypeStruct((2, nc // 4, LAGS, nc), BF),
        ),
        in_specs=[pl.BlockSpec(memory_space=pltpu.SMEM), vmem, vmem]
        + [pl.BlockSpec(memory_space=pl.ANY)] * len(mates),
        out_specs=(vmem, vmem),
        scratch_shapes=[
            pltpu.VMEM((nf, nk, nc), BF),
            pltpu.VMEM((2 * nf, nc, nc), BF),
            pltpu.SemaphoreType.DMA,
        ],
        cost_estimate=pl.CostEstimate(
            flops=8_000_000_000, bytes_accessed=12_000_000, transcendentals=0
        ),
        compiler_params=pltpu.CompilerParams(vmem_limit_bytes=40 * 2**20),
        name="correlate",
    )(info, lhs, table, *mates)


CHAIN = 4
PARTS = 4
AHEAD = 2
ARRIVAL = (
    ((0, 1), (1, 0), (1, 1), (2, 0), (3, 0), (2, 1), (3, 1)),
    ((1, 1), (0, 0), (2, 0), (0, 1), (3, 0), (2, 1), (3, 1)),
    ((2, 1), (3, 0), (1, 0), (3, 1), (0, 0), (1, 1), (0, 1)),
    ((3, 1), (2, 0), (2, 1), (1, 0), (0, 0), (1, 1), (0, 1)),
)
STEPS = 15
TURN_AFTER = {8: (0,), 12: (1, 2), 14: (3,)}
EARLY, EARLY_STEP = (0, 2), 13


def plan_links():
    last = CHAIN - 1
    queue = {}
    for c in range(CHAIN):
        down = [(b, 0, h) for b in range(c, CHAIN) for h in range(PARTS)] + [(last, 1, h) for h in (2, 3)]
        up = [(b, 0, h) for b in range(c, -1, -1) for h in range(PARTS)] + [(0, 1, h) for h in (2, 3)]
        if c > 0:
            queue[c, "down"] = down
        if c < last:
            queue[c, "up"] = up
        near = [b for b in (range(c + 1, CHAIN) if c == 0 else range(c - 1, -1, -1))]
        if c == 1:
            near = [0, 2, 3]
        if c == 2:
            near = [3, 1, 0]
        swap = [(c, 0, h) for h in range(PARTS)]
        for b in near:
            by_chain = (b == last and c < last) or (b == 0 and c > 0)
            swap += [(b, 0, h) for h in range(PARTS) if not (by_chain and h >= 2)]
        queue[c, "swap"] = swap
    have = {(c, (c, 0, h)): 0 for c in range(CHAIN) for h in range(PARTS)}
    start = {key: [] for key in queue}
    for t in range(STEPS):
        new = {}
        for (c, way), items in queue.items():
            at = len(start[c, way])
            if at < len(items) and have.get((c, items[at]), 99) <= t:
                start[c, way].append(t)
                b, sw, h = items[at]
                if way == "swap":
                    new[c, (b, 1 - sw, h)] = t + 1
                else:
                    new[c + (1 if way == "up" else -1), (b, sw, h)] = t + 1
        for key, when in new.items():
            assert key not in have
            have[key] = when
    waits = {(c, t): [] for c in range(CHAIN) for t in range(STEPS)}
    sends = {(c, t): [] for c in range(CHAIN) for t in range(STEPS)}
    for (c, item), when in have.items():
        if when > 0:
            waits[c, when].append(item)
    for (c, way), items in queue.items():
        assert len(start[c, way]) == len(items)
        for item, t in zip(items, start[c, way]):
            sends[c, max(t - AHEAD, have[c, item], 0)].append((way, item))
    for c in range(CHAIN):
        for k in range(ROUNDS):
            step = [t for t, turns in TURN_AFTER.items() if k in turns][0]
            for b, sw in ARRIVAL[c][k : k + 4]:
                for h in range(PARTS):
                    early = k == ROUNDS - 1 and h in EARLY
                    assert have[c, (b, sw, h)] <= (EARLY_STEP if early else step)
    return waits, sends


def fused_kernel(
    pick_ref, spec_ref, order_ref, table_ref, out_ref,
    blocks, lhs, cross, perm, keep, give, beside, passed, across,
    swap_sem, chain_sem, got_sem, give_sem, beside_sem, passed_sem, across_sem,
):
    nf, _, nw, nc = spec_ref.shape
    part = nf // PARTS
    share = nc // 4
    lag_rows = share * LAGS
    pair = lax.axis_index("pair")
    win = lax.axis_index("win")
    c, x = pair // 2, pair % 2
    row, core = win // 2, win % 2
    swap_to = {"pair": pair + 1 - 2 * x}
    core_to = {"win": win + 1 - 2 * core}
    row_to = {"win": win + 2 - 4 * row}
    waits, sends = plan_links()

    def signal(to):
        pl.semaphore_signal(
            pltpu.get_barrier_semaphore(), inc=1, device_id=to,
            device_id_type=pl.DeviceIdType.MESH,
        )

    signal(swap_to)
    signal(core_to)
    signal(row_to)

    @pl.when(c > 0)
    def _():
        signal({"pair": pair - 2})

    @pl.when(c < CHAIN - 1)
    def _():
        signal({"pair": pair + 2})

    def greet():
        @pl.when((c > 0) & (c < CHAIN - 1))
        def _():
            pl.semaphore_wait(pltpu.get_barrier_semaphore(), 5)

        @pl.when((c == 0) | (c == CHAIN - 1))
        def _():
            pl.semaphore_wait(pltpu.get_barrier_semaphore(), 4)

    def copy(way, item):
        b, sw, h = item
        q = 2 * b + (x if sw == 0 else 1 - x)
        ref = blocks.at[q, pl.ds(h * part, part)]
        if way == "swap":
            sem, to = swap_sem.at[b, h], swap_to
        else:
            side = 0 if way == "down" else 1
            sem = chain_sem.at[side, 2 * b + sw, h]
            to = {"pair": pair - 2 if way == "down" else pair + 2}
        return pltpu.make_async_remote_copy(
            src_ref=ref, dst_ref=ref, send_sem=sem, recv_sem=got_sem.at[q, h],
            device_id=to, device_id_type=pl.DeviceIdType.MESH,
        )

    def links(t, only=None):
        for cs in range(CHAIN):

            @pl.when(c == cs)
            def _(cs=cs):
                if only in (None, 0):
                    for item in waits[cs, t]:
                        copy("swap", item).wait_recv()
                for way, item in sends[cs, t]:
                    if only is None or item[2] == only:
                        copy(way, item).start()

    def square(f, carry):
        re = spec_ref[f, 0].astype(F32)
        im = spec_ref[f, 1].astype(F32)
        out_ref[pl.ds(pl.multiple_of((f + 2) * nw, 8), nw)] = re * re + im * im
        return carry

    zero = jnp.zeros((nw, nc), F32)
    for edge in (0, 1, nf + 2, nf + 3):
        out_ref[pl.ds(edge * nw, nw)] = zero
    lax.fori_loop(0, nf, square, 0, unroll=4)
    rows = lax.broadcasted_iota(jnp.int32, (nc, nc), 0)
    cols = lax.broadcasted_iota(jnp.int32, (nc, nc), 1)
    perm[0] = (rows == order_ref[...]).astype(F32).astype(BF)
    perm[1] = (rows == cols).astype(F32).astype(BF)

    def scale(f, carry):
        total = out_ref[pl.ds(pl.multiple_of(f * nw, 8), nw)]
        for d in range(1, 5):
            total += out_ref[pl.ds(pl.multiple_of((f + d) * nw, 8), nw)]
        count = jnp.minimum(f + 2, nf - 1) - jnp.maximum(f - 2, 0) + 1
        mean = total / count.astype(F32)
        inv = 1.0 / jnp.maximum(jnp.sqrt(mean), 0.5)
        white = jnp.concatenate(
            [
                (spec_ref[f, 0].astype(F32) * inv).astype(BF),
                (spec_ref[f, 1].astype(F32) * inv).astype(BF),
            ],
            0,
        )
        blocks[pair, f] = jnp.dot(white, perm[0], preferred_element_type=F32).astype(BF)
        return carry

    greet()
    for h in range(PARTS):
        lax.fori_loop(h * part, (h + 1) * part, scale, 0, unroll=4)
        links(0, h)

    def turn_bin(f, carry):
        turned = lax.dot_general(
            perm[1], blocks[pair, f], (((1,), (1,)), ((), ())), preferred_element_type=F32
        )
        lhs[f] = turned.astype(BF)
        return carry

    lax.fori_loop(0, nf, turn_bin, 0, unroll=4)

    def to_core(k, half):
        at = pl.ds(half * lag_rows, lag_rows)
        return pltpu.make_async_remote_copy(
            src_ref=give.at[k % 2, at], dst_ref=beside.at[k, at],
            send_sem=give_sem.at[k, half], recv_sem=beside_sem.at[k, half],
            device_id=core_to, device_id_type=pl.DeviceIdType.MESH,
        )

    def to_row(k):
        return pltpu.make_async_remote_copy(
            src_ref=passed.at[k], dst_ref=across.at[k], send_sem=passed_sem.at[k],
            recv_sem=across_sem.at[k], device_id=row_to,
            device_id_type=pl.DeviceIdType.MESH,
        )

    def cross_turn(k, parts):
        places = []
        for m in range(4):
            at = jnp.int32(0)
            for cs in range(CHAIN):
                b, sw = ARRIVAL[cs][k + m]
                at = at + (c == cs).astype(jnp.int32) * (2 * b + (x if sw == 0 else 1 - x))
            places.append(at)

        def one_bin(f, carry):
            right = None
            for m in range(4):
                weight = (pick_ref[k] == m).astype(F32)
                term = blocks[places[m], f] * jnp.full((1, nc), weight, F32).astype(BF)
                right = term if right is None else right + term
            turned = jnp.concatenate([right[nw:], -right[:nw]], 0)
            left = lhs[f]
            cross[f] = jnp.dot(left, right, preferred_element_type=F32).astype(BF)
            cross[nf + f] = jnp.dot(left, turned, preferred_element_type=F32).astype(BF)
            return carry

        for h in parts:
            lax.fori_loop(h * part, (h + 1) * part, one_bin, 0, unroll=4)

    def lag_turn(k):
        if k >= 2:
            for half in range(2):
                to_core(k - 2, half).wait_send()

        def lags_of(half, other, u):
            owner = lax.rem(row + half, 2) * 2 + lax.rem(core + other, 2)
            start = pl.multiple_of(owner * share + u * GROUP, GROUP)
            right = cross[:, pl.ds(start, GROUP), :].reshape(2 * nf * GROUP, nc)
            return jnp.dot(table_ref[...], right, preferred_element_type=F32)

        size = GROUP * LAGS

        def send_group(half, u, carry):
            at = pl.multiple_of(half * lag_rows + u * size, size)
            give[k % 2, pl.ds(at, size)] = lags_of(half, 1, u).astype(BF)
            return carry

        def keep_group(half, u, carry):
            if half == 1:
                keep[pl.ds(pl.multiple_of(u * size, size), size)] = lags_of(1, 0, u)
            else:
                to = pl.multiple_of(k * lag_rows + u * size, size)
                out_ref[pl.ds(to, size)] = lags_of(0, 0, u)
            return carry

        groups = share // GROUP
        for half in (1, 0):
            lax.fori_loop(0, groups, functools.partial(send_group, half), 0, unroll=2)
            to_core(k, half).start()
            lax.fori_loop(0, groups, functools.partial(keep_group, half), 0, unroll=2)
            to_core(k, half).wait_recv()
            got = beside[k, pl.ds(half * lag_rows, lag_rows)].astype(F32)
            if half == 1:
                passed[k] = (keep[...] + got).astype(BF)
                to_row(k).start()
            else:
                out_ref[pl.ds(k * lag_rows, lag_rows)] += got

    for t in range(1, STEPS):
        links(t)
        for k in TURN_AFTER.get(t, ()):
            late = k == ROUNDS - 1
            cross_turn(k, [h for h in range(PARTS) if not (late and h in EARLY)])
            lag_turn(k)
        if t == EARLY_STEP:
            cross_turn(ROUNDS - 1, EARLY)
    for k in range(ROUNDS):
        to_row(k).wait_recv()
        out_ref[pl.ds(k * lag_rows, lag_rows)] += across[k].astype(F32)
    for k in range(ROUNDS):
        if k >= 2:
            for half in range(2):
                to_core(k, half).wait_send()
        to_row(k).wait_send()
    for cs in range(CHAIN):

        @pl.when(c == cs)
        def _(cs=cs):
            for t in range(STEPS):
                for way, item in sends[cs, t]:
                    copy(way, item).wait_send()


def fused(pick, spectra, order, table):
    nf, _, nw, nc = spectra.shape
    blocks = lax.axis_size("pair")
    rows = nc // 4 * LAGS
    vmem = pl.BlockSpec(memory_space=pltpu.VMEM)
    dma = pltpu.SemaphoreType.DMA
    return pl.pallas_call(
        fused_kernel,
        out_shape=jax.ShapeDtypeStruct((ROUNDS * rows, nc), F32),
        in_specs=[pl.BlockSpec(memory_space=pltpu.SMEM), vmem, vmem, vmem],
        out_specs=vmem,
        scratch_shapes=[
            pltpu.VMEM((blocks, nf, 2 * nw, nc), BF),
            pltpu.VMEM((nf, nc, 2 * nw), BF),
            pltpu.VMEM((2 * nf, nc, nc), BF),
            pltpu.VMEM((2, nc, nc), BF),
            pltpu.VMEM((rows, nc), F32),
            pltpu.VMEM((2, 2 * rows, nc), BF),
            pltpu.VMEM((ROUNDS, 2 * rows, nc), BF),
            pltpu.VMEM((ROUNDS, rows, nc), BF),
            pltpu.VMEM((ROUNDS, rows, nc), BF),
            dma((CHAIN, PARTS)),
            dma((2, 2 * CHAIN, PARTS)),
            dma((blocks, PARTS)),
            dma((ROUNDS, 2)),
            dma((ROUNDS, 2)),
            dma((ROUNDS,)),
            dma((ROUNDS,)),
        ],
        cost_estimate=pl.CostEstimate(
            flops=16_000_000_000, bytes_accessed=16_000_000, transcendentals=0
        ),
        compiler_params=pltpu.CompilerParams(
            vmem_limit_bytes=60 * 2**20, collective_id=0, has_side_effects=True
        ),
        name="fused",
    )(pick, spectra, order, table)


def arrange_kernel(place_ref, sums_ref, out_ref, held, in_sem, out_sem):
    rounds, rows = held.shape[:2]
    half = rows // 2
    for r in range(rounds):
        for h in range(2):
            at = pl.ds(h * half, half)
            pltpu.make_async_copy(
                sums_ref.at[place_ref[r], at], held.at[r, at], in_sem.at[r, h]
            ).start()
    for step in ("move", "finish"):
        for r in range(rounds):
            for h in range(2):
                at = pl.ds(h * half, half)
                out = pltpu.make_async_copy(held.at[r, at], out_ref.at[at, r], out_sem.at[r, h])
                if step == "move":
                    pltpu.make_async_copy(
                        sums_ref.at[place_ref[r], at], held.at[r, at], in_sem.at[r, h]
                    ).wait()
                    out.start()
                else:
                    out.wait()


def arrange(place, sums):
    rounds, rows, lags, nc = sums.shape
    return pl.pallas_call(
        arrange_kernel,
        in_specs=[
            pl.BlockSpec(memory_space=pltpu.SMEM),
            pl.BlockSpec(memory_space=pl.ANY),
        ],
        out_specs=pl.BlockSpec(memory_space=pl.ANY),
        out_shape=jax.ShapeDtypeStruct((rows, rounds, lags, nc), F32),
        scratch_shapes=[
            pltpu.VMEM((rounds, rows, lags, nc), F32),
            pltpu.SemaphoreType.DMA((rounds, 2)),
            pltpu.SemaphoreType.DMA((rounds, 2)),
        ],
        name="arrange",
    )(place, sums)


def local(spectra, channel_order, partners):
    num_blocks = lax.axis_size("pair")
    win_count = lax.axis_size("win")
    nf, _, nw, nc = spectra.shape
    spread = jnp.asarray(make_table(nf, LAGS, nw * win_count))
    me = lax.axis_index("pair")
    win = lax.axis_index("win")
    if num_blocks == 2 * CHAIN and win_count == 4:
        mine = partners[:, me]
        rank = jnp.zeros_like(mine)
        for c in range(CHAIN):
            for index, (b, sw) in enumerate(ARRIVAL[c]):
                same = (mine // 2 == b) & ((mine % 2 != me % 2) == (sw == 1))
                rank = jnp.where((me // 2 == c) & same, index, rank)
        place = jnp.sum((rank[None, :] < rank[:, None]).astype(jnp.int32), 1)
        turns = jnp.arange(ROUNDS, dtype=jnp.int32)
        pick = jnp.sum(jnp.where(place[None, :] == turns[:, None], rank[None, :], 0), 1) - turns
        sums = fused(pick.astype(jnp.int32), spectra, channel_order, spread)
        return arrange(place, sums.reshape(ROUNDS, nc // 4, LAGS, nc))[None]
    own, lhs = whiten(spectra, channel_order)
    row, core = win // 2, win % 2
    results = []
    turned = lax.all_to_all(
        own.reshape(num_blocks, -1), "pair", split_axis=0, concat_axis=0, tiled=True
    )
    for turn in range(ROUNDS):
        arranged = jnp.take(turned, partners[turn], axis=0)
        received = lax.all_to_all(arranged, "pair", split_axis=0, concat_axis=0, tiled=True)
        info = jnp.stack([jnp.int32(0), core, row]).astype(jnp.int32)
        keep, give = correlate(info, lhs, spread, [received.reshape(own.shape)])
        beside = lax.ppermute(give, "win", [(w, w ^ 1) for w in range(win_count)])
        passed = (keep[1] + beside[1].astype(F32)).astype(BF)
        across = lax.ppermute(passed, "win", [(w, w ^ 2) for w in range(win_count)])
        results.append(keep[0] + beside[0].astype(F32) + across.astype(F32))
    return jnp.stack(results, 1)[None]


def solution(mesh):
    return jax.shard_map(
        local,
        mesh=mesh,
        in_specs=(P(None, None, "win", "pair"), P("pair", None), P()),
        out_specs=P("pair", "win", None, None, None),
        check_vma=False,
    )
```

```python
import functools
import math

import jax
import jax.numpy as jnp
import ml_dtypes
import numpy as np
from jax import lax
from jax.experimental import pallas as pl
from jax.experimental.pallas import tpu as pltpu
from jax.sharding import PartitionSpec as P

LAGS = 16
ROUNDS = 4
GROUP = 16
BF = jnp.bfloat16
F32 = jnp.float32


def make_table(num_bins, num_lags, window_total):
    bin_freq = np.arange(num_bins, dtype=np.float64)[:, None]
    lag_index = (np.arange(num_lags) - num_lags // 2).astype(np.float64)[None, :]
    phase_angle = math.pi * bin_freq * lag_index / num_bins
    norm_factor = 1.0 / math.sqrt(window_total * num_bins)
    table = np.concatenate([np.cos(phase_angle), -np.sin(phase_angle)], 0) * norm_factor
    spread = table.T[None, :, :, None] * np.eye(GROUP)[:, None, None, :]
    return spread.reshape(GROUP * num_lags, 2 * num_bins * GROUP).astype(ml_dtypes.bfloat16)


def whiten_kernel(spec_ref, order_ref, own_ref, lhs_ref, power):
    nf, _, nw, nc = spec_ref.shape
    zero = jnp.zeros((nw, nc), F32)
    for edge in (0, 1, nf + 2, nf + 3):
        power[edge] = zero

    def square(f, carry):
        re = spec_ref[f, 0].astype(F32)
        im = spec_ref[f, 1].astype(F32)
        power[f + 2] = re * re + im * im
        return carry

    lax.fori_loop(0, nf, square, 0, unroll=4)
    rows = lax.broadcasted_iota(jnp.int32, (nc, nc), 0)
    cols = lax.broadcasted_iota(jnp.int32, (nc, nc), 1)
    pick = (rows == order_ref[...]).astype(F32).astype(BF)
    eye = (rows == cols).astype(F32).astype(BF)

    def scale(f, carry):
        total = power[f] + power[f + 1] + power[f + 2] + power[f + 3] + power[f + 4]
        count = jnp.minimum(f + 2, nf - 1) - jnp.maximum(f - 2, 0) + 1
        mean = total / count.astype(F32)
        inv = 1.0 / jnp.maximum(jnp.sqrt(mean), 0.5)
        white = jnp.concatenate(
            [
                (spec_ref[f, 0].astype(F32) * inv).astype(BF),
                (spec_ref[f, 1].astype(F32) * inv).astype(BF),
            ],
            0,
        )
        own = jnp.dot(white, pick, preferred_element_type=F32).astype(BF)
        own_ref[f] = own
        turned = lax.dot_general(eye, own, (((1,), (1,)), ((), ())), preferred_element_type=F32)
        lhs_ref[f] = turned.astype(BF)
        return carry

    lax.fori_loop(0, nf, scale, 0)


def whiten(spectra, order):
    nf, _, nw, nc = spectra.shape
    vmem = pl.BlockSpec(memory_space=pltpu.VMEM)
    return pl.pallas_call(
        whiten_kernel,
        out_shape=(
            jax.ShapeDtypeStruct((nf, 2 * nw, nc), BF),
            jax.ShapeDtypeStruct((nf, nc, 2 * nw), BF),
        ),
        in_specs=[vmem, vmem],
        out_specs=(vmem, vmem),
        scratch_shapes=[pltpu.VMEM((nf + 4, nw, nc), F32)],
        compiler_params=pltpu.CompilerParams(vmem_limit_bytes=40 * 2**20),
        name="whiten",
    )(spectra, order)


def corr_kernel(info_ref, lhs_ref, table_ref, *refs):
    mates = refs[:-5]
    keep_ref, send_ref, mate, cross, sem = refs[-5:]
    nf, nk, nc = mate.shape
    nw = nk // 2
    slot, core, row = info_ref[0], info_ref[1], info_ref[2]
    for s, ref in enumerate(mates):

        @pl.when(slot == s)
        def _(ref=ref):
            pltpu.make_async_copy(ref, mate, sem).start()

    pltpu.make_async_copy(mates[0], mate, sem).wait()

    def one_bin(f, carry):
        right = mate[f]
        turned = jnp.concatenate([right[nw:], -right[:nw]], 0)
        left = lhs_ref[f]
        cross[f] = jnp.dot(left, right, preferred_element_type=F32).astype(BF)
        cross[nf + f] = jnp.dot(left, turned, preferred_element_type=F32).astype(BF)
        return carry

    lax.fori_loop(0, nf, one_bin, 0)
    share = keep_ref.shape[1]
    per = share // GROUP

    def one_group(step, carry):
        half, u = step // per, step % per
        for other, out_ref in ((0, keep_ref), (1, send_ref)):
            owner = lax.rem(row + half, 2) * 2 + lax.rem(core + other, 2)
            start = pl.multiple_of(owner * share + u * GROUP, GROUP)
            right = cross[:, pl.ds(start, GROUP), :].reshape(2 * nf * GROUP, nc)
            lags = jnp.dot(table_ref[...], right, preferred_element_type=F32)
            at = pl.multiple_of(u * GROUP, GROUP)
            out_ref[half, pl.ds(at, GROUP)] = lags.reshape(GROUP, LAGS, nc).astype(out_ref.dtype)
        return carry

    lax.fori_loop(0, 2 * per, one_group, 0)


def correlate(info, lhs, table, mates):
    nf, nc, nk = lhs.shape
    vmem = pl.BlockSpec(memory_space=pltpu.VMEM)
    return pl.pallas_call(
        corr_kernel,
        out_shape=(
            jax.ShapeDtypeStruct((2, nc // 4, LAGS, nc), F32),
            jax.ShapeDtypeStruct((2, nc // 4, LAGS, nc), BF),
        ),
        in_specs=[pl.BlockSpec(memory_space=pltpu.SMEM), vmem, vmem]
        + [pl.BlockSpec(memory_space=pl.ANY)] * len(mates),
        out_specs=(vmem, vmem),
        scratch_shapes=[
            pltpu.VMEM((nf, nk, nc), BF),
            pltpu.VMEM((2 * nf, nc, nc), BF),
            pltpu.SemaphoreType.DMA,
        ],
        cost_estimate=pl.CostEstimate(
            flops=8_000_000_000, bytes_accessed=12_000_000, transcendentals=0
        ),
        compiler_params=pltpu.CompilerParams(vmem_limit_bytes=40 * 2**20),
        name="correlate",
    )(info, lhs, table, *mates)


CHAIN = 4
PARTS = 4
AHEAD = 2
ARRIVAL = (
    ((0, 1), (1, 0), (1, 1), (2, 0), (3, 0), (2, 1), (3, 1)),
    ((1, 1), (0, 0), (2, 0), (0, 1), (3, 0), (2, 1), (3, 1)),
    ((2, 1), (3, 0), (1, 0), (3, 1), (0, 0), (1, 1), (0, 1)),
    ((3, 1), (2, 0), (2, 1), (1, 0), (0, 0), (1, 1), (0, 1)),
)
STEPS = 15
TURN_AFTER = {8: (0,), 12: (1, 2), 14: (3,)}
EARLY, EARLY_STEP = (0, 2), 13


def plan_links():
    last = CHAIN - 1
    queue = {}
    for c in range(CHAIN):
        down = [(b, 0, h) for b in range(c, CHAIN) for h in range(PARTS)] + [(last, 1, h) for h in (2, 3)]
        up = [(b, 0, h) for b in range(c, -1, -1) for h in range(PARTS)] + [(0, 1, h) for h in (2, 3)]
        if c > 0:
            queue[c, "down"] = down
        if c < last:
            queue[c, "up"] = up
        near = [b for b in (range(c + 1, CHAIN) if c == 0 else range(c - 1, -1, -1))]
        if c == 1:
            near = [0, 2, 3]
        if c == 2:
            near = [3, 1, 0]
        swap = [(c, 0, h) for h in range(PARTS)]
        for b in near:
            by_chain = (b == last and c < last) or (b == 0 and c > 0)
            swap += [(b, 0, h) for h in range(PARTS) if not (by_chain and h >= 2)]
        queue[c, "swap"] = swap
    have = {(c, (c, 0, h)): 0 for c in range(CHAIN) for h in range(PARTS)}
    start = {key: [] for key in queue}
    for t in range(STEPS):
        new = {}
        for (c, way), items in queue.items():
            at = len(start[c, way])
            if at < len(items) and have.get((c, items[at]), 99) <= t:
                start[c, way].append(t)
                b, sw, h = items[at]
                if way == "swap":
                    new[c, (b, 1 - sw, h)] = t + 1
                else:
                    new[c + (1 if way == "up" else -1), (b, sw, h)] = t + 1
        for key, when in new.items():
            assert key not in have
            have[key] = when
    waits = {(c, t): [] for c in range(CHAIN) for t in range(STEPS)}
    sends = {(c, t): [] for c in range(CHAIN) for t in range(STEPS)}
    for (c, item), when in have.items():
        if when > 0:
            waits[c, when].append(item)
    for (c, way), items in queue.items():
        assert len(start[c, way]) == len(items)
        for item, t in zip(items, start[c, way]):
            sends[c, max(t - AHEAD, have[c, item], 0)].append((way, item))
    for c in range(CHAIN):
        for k in range(ROUNDS):
            step = [t for t, turns in TURN_AFTER.items() if k in turns][0]
            for b, sw in ARRIVAL[c][k : k + 4]:
                for h in range(PARTS):
                    early = k == ROUNDS - 1 and h in EARLY
                    assert have[c, (b, sw, h)] <= (EARLY_STEP if early else step)
    return waits, sends


def fused_kernel(
    pick_ref, spec_ref, order_ref, table_ref, out_ref,
    blocks, lhs, cross, perm, keep, give, beside, passed, across,
    swap_sem, chain_sem, got_sem, give_sem, beside_sem, passed_sem, across_sem,
):
    nf, _, nw, nc = spec_ref.shape
    part = nf // PARTS
    share = nc // 4
    lag_rows = share * LAGS
    pair = lax.axis_index("pair")
    win = lax.axis_index("win")
    c, x = pair // 2, pair % 2
    row, core = win // 2, win % 2
    swap_to = {"pair": pair + 1 - 2 * x}
    core_to = {"win": win + 1 - 2 * core}
    row_to = {"win": win + 2 - 4 * row}
    waits, sends = plan_links()

    def signal(to):
        pl.semaphore_signal(
            pltpu.get_barrier_semaphore(), inc=1, device_id=to,
            device_id_type=pl.DeviceIdType.MESH,
        )

    signal(swap_to)
    signal(core_to)
    signal(row_to)

    @pl.when(c > 0)
    def _():
        signal({"pair": pair - 2})

    @pl.when(c < CHAIN - 1)
    def _():
        signal({"pair": pair + 2})

    def greet():
        @pl.when((c > 0) & (c < CHAIN - 1))
        def _():
            pl.semaphore_wait(pltpu.get_barrier_semaphore(), 5)

        @pl.when((c == 0) | (c == CHAIN - 1))
        def _():
            pl.semaphore_wait(pltpu.get_barrier_semaphore(), 4)

    def copy(way, item):
        b, sw, h = item
        q = 2 * b + (x if sw == 0 else 1 - x)
        ref = blocks.at[q, pl.ds(h * part, part)]
        if way == "swap":
            sem, to = swap_sem.at[b, h], swap_to
        else:
            side = 0 if way == "down" else 1
            sem = chain_sem.at[side, 2 * b + sw, h]
            to = {"pair": pair - 2 if way == "down" else pair + 2}
        return pltpu.make_async_remote_copy(
            src_ref=ref, dst_ref=ref, send_sem=sem, recv_sem=got_sem.at[q, h],
            device_id=to, device_id_type=pl.DeviceIdType.MESH,
        )

    def links(t, only=None):
        for cs in range(CHAIN):

            @pl.when(c == cs)
            def _(cs=cs):
                if only in (None, 0):
                    for item in waits[cs, t]:
                        copy("swap", item).wait_recv()
                for way, item in sends[cs, t]:
                    if only is None or item[2] == only:
                        copy(way, item).start()

    def square(f, carry):
        re = spec_ref[f, 0].astype(F32)
        im = spec_ref[f, 1].astype(F32)
        out_ref[pl.ds(pl.multiple_of((f + 2) * nw, 8), nw)] = re * re + im * im
        return carry

    zero = jnp.zeros((nw, nc), F32)
    for edge in (0, 1, nf + 2, nf + 3):
        out_ref[pl.ds(edge * nw, nw)] = zero
    lax.fori_loop(0, part + 2, square, 0, unroll=5)
    rows = lax.broadcasted_iota(jnp.int32, (nc, nc), 0)
    cols = lax.broadcasted_iota(jnp.int32, (nc, nc), 1)
    perm[0] = (rows == order_ref[...]).astype(F32).astype(BF)
    perm[1] = (rows == cols).astype(F32).astype(BF)

    def scale(f, carry):
        total = out_ref[pl.ds(pl.multiple_of(f * nw, 8), nw)]
        for d in range(1, 5):
            total += out_ref[pl.ds(pl.multiple_of((f + d) * nw, 8), nw)]
        count = jnp.minimum(f + 2, nf - 1) - jnp.maximum(f - 2, 0) + 1
        mean = total / count.astype(F32)
        inv = 1.0 / jnp.maximum(jnp.sqrt(mean), 0.5)
        white = jnp.concatenate(
            [
                (spec_ref[f, 0].astype(F32) * inv).astype(BF),
                (spec_ref[f, 1].astype(F32) * inv).astype(BF),
            ],
            0,
        )
        blocks[pair, f] = jnp.dot(white, perm[0], preferred_element_type=F32).astype(BF)
        return carry

    greet()
    for h in range(PARTS):
        lax.fori_loop(h * part, (h + 1) * part, scale, 0, unroll=4)
        links(0, h)
        if h == 0:
            lax.fori_loop(part + 2, nf, square, 0, unroll=2)

    def turn_bin(f, carry):
        turned = lax.dot_general(
            perm[1], blocks[pair, f], (((1,), (1,)), ((), ())), preferred_element_type=F32
        )
        lhs[f] = turned.astype(BF)
        return carry

    lax.fori_loop(0, nf, turn_bin, 0, unroll=4)

    piece_rows = lag_rows // 2

    def to_core(k, half, piece):
        at = pl.ds(half * lag_rows + piece * piece_rows, piece_rows)
        return pltpu.make_async_remote_copy(
            src_ref=give.at[k % 2, at], dst_ref=beside.at[k, at],
            send_sem=give_sem.at[k, half, piece], recv_sem=beside_sem.at[k, half, piece],
            device_id=core_to, device_id_type=pl.DeviceIdType.MESH,
        )

    def to_row(k, piece):
        at = pl.ds(piece * piece_rows, piece_rows)
        return pltpu.make_async_remote_copy(
            src_ref=passed.at[k, at], dst_ref=across.at[k, at],
            send_sem=passed_sem.at[k, piece], recv_sem=across_sem.at[k, piece],
            device_id=row_to, device_id_type=pl.DeviceIdType.MESH,
        )

    def cross_turn(k, parts):
        places = []
        for m in range(4):
            at = jnp.int32(0)
            for cs in range(CHAIN):
                b, sw = ARRIVAL[cs][k + m]
                at = at + (c == cs).astype(jnp.int32) * (2 * b + (x if sw == 0 else 1 - x))
            places.append(at)

        def one_bin(f, carry):
            right = None
            for m in range(4):
                weight = (pick_ref[k] == m).astype(F32)
                term = blocks[places[m], f] * jnp.full((1, nc), weight, F32).astype(BF)
                right = term if right is None else right + term
            turned = jnp.concatenate([right[nw:], -right[:nw]], 0)
            left = lhs[f]
            cross[f] = jnp.dot(left, right, preferred_element_type=F32).astype(BF)
            cross[nf + f] = jnp.dot(left, turned, preferred_element_type=F32).astype(BF)
            return carry

        for h in parts:
            lax.fori_loop(h * part, (h + 1) * part, one_bin, 0, unroll=4)

    def lag_turn(k):
        if k >= 2:
            for half in range(2):
                for piece in range(2):
                    to_core(k - 2, half, piece).wait_send()

        def lags_of(half, other, u):
            owner = lax.rem(row + half, 2) * 2 + lax.rem(core + other, 2)
            start = pl.multiple_of(owner * share + u * GROUP, GROUP)
            right = cross[:, pl.ds(start, GROUP), :].reshape(2 * nf * GROUP, nc)
            return jnp.dot(table_ref[...], right, preferred_element_type=F32)

        size = GROUP * LAGS

        def send_group(half, u, carry):
            at = pl.multiple_of(half * lag_rows + u * size, size)
            give[k % 2, pl.ds(at, size)] = lags_of(half, 1, u).astype(BF)
            return carry

        def keep_group(half, u, carry):
            if half == 1:
                keep[pl.ds(pl.multiple_of(u * size, size), size)] = lags_of(1, 0, u)
            else:
                to = pl.multiple_of(k * lag_rows + u * size, size)
                out_ref[pl.ds(to, size)] = lags_of(0, 0, u)
            return carry

        groups = share // GROUP // 2

        def receive(half, piece):
            to_core(k, half, piece).wait_recv()
            at = half * lag_rows + piece * piece_rows
            return beside[k, pl.ds(at, piece_rows)].astype(F32)

        for half in (1, 0):
            for piece in range(2):
                first, last = piece * groups, (piece + 1) * groups
                lax.fori_loop(first, last, functools.partial(send_group, half), 0, unroll=2)
                to_core(k, half, piece).start()
                lax.fori_loop(first, last, functools.partial(keep_group, half), 0, unroll=2)
                if half == 1:
                    at = pl.ds(piece * piece_rows, piece_rows)
                    passed[k, at] = (keep[at] + receive(half, piece)).astype(BF)
                    to_row(k, piece).start()
        for piece in range(2):
            at = pl.ds(k * lag_rows + piece * piece_rows, piece_rows)
            out_ref[at] += receive(0, piece)

    for t in range(1, STEPS):
        links(t)
        for k in TURN_AFTER.get(t, ()):
            late = k == ROUNDS - 1
            cross_turn(k, [h for h in range(PARTS) if not (late and h in EARLY)])
            lag_turn(k)
        if t == EARLY_STEP:
            cross_turn(ROUNDS - 1, EARLY)
    for k in range(ROUNDS):
        for piece in range(2):
            to_row(k, piece).wait_recv()
            at = pl.ds(k * lag_rows + piece * piece_rows, piece_rows)
            out_ref[at] += across[k, pl.ds(piece * piece_rows, piece_rows)].astype(F32)
    for k in range(ROUNDS):
        for piece in range(2):
            if k >= 2:
                for half in range(2):
                    to_core(k, half, piece).wait_send()
            to_row(k, piece).wait_send()
    for cs in range(CHAIN):

        @pl.when(c == cs)
        def _(cs=cs):
            for t in range(STEPS):
                for way, item in sends[cs, t]:
                    copy(way, item).wait_send()


def fused(pick, spectra, order, table):
    nf, _, nw, nc = spectra.shape
    blocks = lax.axis_size("pair")
    rows = nc // 4 * LAGS
    vmem = pl.BlockSpec(memory_space=pltpu.VMEM)
    dma = pltpu.SemaphoreType.DMA
    return pl.pallas_call(
        fused_kernel,
        out_shape=jax.ShapeDtypeStruct((ROUNDS * rows, nc), F32),
        in_specs=[pl.BlockSpec(memory_space=pltpu.SMEM), vmem, vmem, vmem],
        out_specs=vmem,
        scratch_shapes=[
            pltpu.VMEM((blocks, nf, 2 * nw, nc), BF),
            pltpu.VMEM((nf, nc, 2 * nw), BF),
            pltpu.VMEM((2 * nf, nc, nc), BF),
            pltpu.VMEM((2, nc, nc), BF),
            pltpu.VMEM((rows, nc), F32),
            pltpu.VMEM((2, 2 * rows, nc), BF),
            pltpu.VMEM((ROUNDS, 2 * rows, nc), BF),
            pltpu.VMEM((ROUNDS, rows, nc), BF),
            pltpu.VMEM((ROUNDS, rows, nc), BF),
            dma((CHAIN, PARTS)),
            dma((2, 2 * CHAIN, PARTS)),
            dma((blocks, PARTS)),
            dma((ROUNDS, 2, 2)),
            dma((ROUNDS, 2, 2)),
            dma((ROUNDS, 2)),
            dma((ROUNDS, 2)),
        ],
        cost_estimate=pl.CostEstimate(
            flops=16_000_000_000, bytes_accessed=16_000_000, transcendentals=0
        ),
        compiler_params=pltpu.CompilerParams(
            vmem_limit_bytes=60 * 2**20, collective_id=0, has_side_effects=True
        ),
        name="fused",
    )(pick, spectra, order, table)


def arrange_kernel(place_ref, sums_ref, out_ref, held, in_sem, out_sem):
    rounds, rows = held.shape[:2]
    half = rows // 2
    for r in range(rounds):
        for h in range(2):
            at = pl.ds(h * half, half)
            pltpu.make_async_copy(
                sums_ref.at[place_ref[r], at], held.at[r, at], in_sem.at[r, h]
            ).start()
    for step in ("move", "finish"):
        for r in range(rounds):
            for h in range(2):
                at = pl.ds(h * half, half)
                out = pltpu.make_async_copy(held.at[r, at], out_ref.at[at, r], out_sem.at[r, h])
                if step == "move":
                    pltpu.make_async_copy(
                        sums_ref.at[place_ref[r], at], held.at[r, at], in_sem.at[r, h]
                    ).wait()
                    out.start()
                else:
                    out.wait()


def arrange(place, sums):
    rounds, rows, lags, nc = sums.shape
    return pl.pallas_call(
        arrange_kernel,
        in_specs=[
            pl.BlockSpec(memory_space=pltpu.SMEM),
            pl.BlockSpec(memory_space=pl.ANY),
        ],
        out_specs=pl.BlockSpec(memory_space=pl.ANY),
        out_shape=jax.ShapeDtypeStruct((rows, rounds, lags, nc), F32),
        scratch_shapes=[
            pltpu.VMEM((rounds, rows, lags, nc), F32),
            pltpu.SemaphoreType.DMA((rounds, 2)),
            pltpu.SemaphoreType.DMA((rounds, 2)),
        ],
        name="arrange",
    )(place, sums)


def local(spectra, channel_order, partners):
    num_blocks = lax.axis_size("pair")
    win_count = lax.axis_size("win")
    nf, _, nw, nc = spectra.shape
    spread = jnp.asarray(make_table(nf, LAGS, nw * win_count))
    me = lax.axis_index("pair")
    win = lax.axis_index("win")
    if num_blocks == 2 * CHAIN and win_count == 4:
        mine = partners[:, me]
        rank = jnp.zeros_like(mine)
        for c in range(CHAIN):
            for index, (b, sw) in enumerate(ARRIVAL[c]):
                same = (mine // 2 == b) & ((mine % 2 != me % 2) == (sw == 1))
                rank = jnp.where((me // 2 == c) & same, index, rank)
        place = jnp.sum((rank[None, :] < rank[:, None]).astype(jnp.int32), 1)
        turns = jnp.arange(ROUNDS, dtype=jnp.int32)
        pick = jnp.sum(jnp.where(place[None, :] == turns[:, None], rank[None, :], 0), 1) - turns
        sums = fused(pick.astype(jnp.int32), spectra, channel_order, spread)
        return arrange(place, sums.reshape(ROUNDS, nc // 4, LAGS, nc))[None]
    own, lhs = whiten(spectra, channel_order)
    row, core = win // 2, win % 2
    results = []
    turned = lax.all_to_all(
        own.reshape(num_blocks, -1), "pair", split_axis=0, concat_axis=0, tiled=True
    )
    for turn in range(ROUNDS):
        arranged = jnp.take(turned, partners[turn], axis=0)
        received = lax.all_to_all(arranged, "pair", split_axis=0, concat_axis=0, tiled=True)
        info = jnp.stack([jnp.int32(0), core, row]).astype(jnp.int32)
        keep, give = correlate(info, lhs, spread, [received.reshape(own.shape)])
        beside = lax.ppermute(give, "win", [(w, w ^ 1) for w in range(win_count)])
        passed = (keep[1] + beside[1].astype(F32)).astype(BF)
        across = lax.ppermute(passed, "win", [(w, w ^ 2) for w in range(win_count)])
        results.append(keep[0] + beside[0].astype(F32) + across.astype(F32))
    return jnp.stack(results, 1)[None]


def solution(mesh):
    return jax.shard_map(
        local,
        mesh=mesh,
        in_specs=(P(None, None, "win", "pair"), P("pair", None), P()),
        out_specs=P("pair", "win", None, None, None),
        check_vma=False,
    )
```

```python
import functools
import math

import jax
import jax.numpy as jnp
import ml_dtypes
import numpy as np
from jax import lax
from jax.experimental import pallas as pl
from jax.experimental.pallas import tpu as pltpu
from jax.sharding import PartitionSpec as P

LAGS = 16
ROUNDS = 4
GROUP = 16
BF = jnp.bfloat16
F32 = jnp.float32


def make_table(num_bins, num_lags, window_total):
    bin_freq = np.arange(num_bins, dtype=np.float64)[:, None]
    lag_index = (np.arange(num_lags) - num_lags // 2).astype(np.float64)[None, :]
    phase_angle = math.pi * bin_freq * lag_index / num_bins
    norm_factor = 1.0 / math.sqrt(window_total * num_bins)
    table = np.concatenate([np.cos(phase_angle), -np.sin(phase_angle)], 0) * norm_factor
    spread = table.T[None, :, :, None] * np.eye(GROUP)[:, None, None, :]
    return spread.reshape(GROUP * num_lags, 2 * num_bins * GROUP).astype(ml_dtypes.bfloat16)


def whiten_kernel(spec_ref, order_ref, own_ref, lhs_ref, power):
    nf, _, nw, nc = spec_ref.shape
    zero = jnp.zeros((nw, nc), F32)
    for edge in (0, 1, nf + 2, nf + 3):
        power[edge] = zero

    def square(f, carry):
        re = spec_ref[f, 0].astype(F32)
        im = spec_ref[f, 1].astype(F32)
        power[f + 2] = re * re + im * im
        return carry

    lax.fori_loop(0, nf, square, 0, unroll=4)
    rows = lax.broadcasted_iota(jnp.int32, (nc, nc), 0)
    cols = lax.broadcasted_iota(jnp.int32, (nc, nc), 1)
    pick = (rows == order_ref[...]).astype(F32).astype(BF)
    eye = (rows == cols).astype(F32).astype(BF)

    def scale(f, carry):
        total = power[f] + power[f + 1] + power[f + 2] + power[f + 3] + power[f + 4]
        count = jnp.minimum(f + 2, nf - 1) - jnp.maximum(f - 2, 0) + 1
        mean = total / count.astype(F32)
        inv = 1.0 / jnp.maximum(jnp.sqrt(mean), 0.5)
        white = jnp.concatenate(
            [
                (spec_ref[f, 0].astype(F32) * inv).astype(BF),
                (spec_ref[f, 1].astype(F32) * inv).astype(BF),
            ],
            0,
        )
        own = jnp.dot(white, pick, preferred_element_type=F32).astype(BF)
        own_ref[f] = own
        turned = lax.dot_general(eye, own, (((1,), (1,)), ((), ())), preferred_element_type=F32)
        lhs_ref[f] = turned.astype(BF)
        return carry

    lax.fori_loop(0, nf, scale, 0)


def whiten(spectra, order):
    nf, _, nw, nc = spectra.shape
    vmem = pl.BlockSpec(memory_space=pltpu.VMEM)
    return pl.pallas_call(
        whiten_kernel,
        out_shape=(
            jax.ShapeDtypeStruct((nf, 2 * nw, nc), BF),
            jax.ShapeDtypeStruct((nf, nc, 2 * nw), BF),
        ),
        in_specs=[vmem, vmem],
        out_specs=(vmem, vmem),
        scratch_shapes=[pltpu.VMEM((nf + 4, nw, nc), F32)],
        compiler_params=pltpu.CompilerParams(vmem_limit_bytes=40 * 2**20),
        name="whiten",
    )(spectra, order)


def corr_kernel(info_ref, lhs_ref, table_ref, *refs):
    mates = refs[:-5]
    keep_ref, send_ref, mate, cross, sem = refs[-5:]
    nf, nk, nc = mate.shape
    nw = nk // 2
    slot, core, row = info_ref[0], info_ref[1], info_ref[2]
    for s, ref in enumerate(mates):

        @pl.when(slot == s)
        def _(ref=ref):
            pltpu.make_async_copy(ref, mate, sem).start()

    pltpu.make_async_copy(mates[0], mate, sem).wait()

    def one_bin(f, carry):
        right = mate[f]
        turned = jnp.concatenate([right[nw:], -right[:nw]], 0)
        left = lhs_ref[f]
        cross[f] = jnp.dot(left, right, preferred_element_type=F32).astype(BF)
        cross[nf + f] = jnp.dot(left, turned, preferred_element_type=F32).astype(BF)
        return carry

    lax.fori_loop(0, nf, one_bin, 0)
    share = keep_ref.shape[1]
    per = share // GROUP

    def one_group(step, carry):
        half, u = step // per, step % per
        for other, out_ref in ((0, keep_ref), (1, send_ref)):
            owner = lax.rem(row + half, 2) * 2 + lax.rem(core + other, 2)
            start = pl.multiple_of(owner * share + u * GROUP, GROUP)
            right = cross[:, pl.ds(start, GROUP), :].reshape(2 * nf * GROUP, nc)
            lags = jnp.dot(table_ref[...], right, preferred_element_type=F32)
            at = pl.multiple_of(u * GROUP, GROUP)
            out_ref[half, pl.ds(at, GROUP)] = lags.reshape(GROUP, LAGS, nc).astype(out_ref.dtype)
        return carry

    lax.fori_loop(0, 2 * per, one_group, 0)


def correlate(info, lhs, table, mates):
    nf, nc, nk = lhs.shape
    vmem = pl.BlockSpec(memory_space=pltpu.VMEM)
    return pl.pallas_call(
        corr_kernel,
        out_shape=(
            jax.ShapeDtypeStruct((2, nc // 4, LAGS, nc), F32),
            jax.ShapeDtypeStruct((2, nc // 4, LAGS, nc), BF),
        ),
        in_specs=[pl.BlockSpec(memory_space=pltpu.SMEM), vmem, vmem]
        + [pl.BlockSpec(memory_space=pl.ANY)] * len(mates),
        out_specs=(vmem, vmem),
        scratch_shapes=[
            pltpu.VMEM((nf, nk, nc), BF),
            pltpu.VMEM((2 * nf, nc, nc), BF),
            pltpu.SemaphoreType.DMA,
        ],
        cost_estimate=pl.CostEstimate(
            flops=8_000_000_000, bytes_accessed=12_000_000, transcendentals=0
        ),
        compiler_params=pltpu.CompilerParams(vmem_limit_bytes=40 * 2**20),
        name="correlate",
    )(info, lhs, table, *mates)


CHAIN = 4
PARTS = 4
ARRIVAL = (
    ((0, 1), (1, 0), (1, 1), (2, 0), (3, 0), (2, 1), (3, 1)),
    ((1, 1), (0, 0), (2, 0), (0, 1), (3, 0), (2, 1), (3, 1)),
    ((2, 1), (3, 0), (1, 0), (3, 1), (0, 0), (1, 1), (0, 1)),
    ((3, 1), (2, 0), (2, 1), (1, 0), (0, 0), (1, 1), (0, 1)),
)
STEPS = 15
TURN_AFTER = {8: (0,), 12: (1, 2), 14: (3,)}
EARLY, EARLY_STEP = (0, 2), 13


def plan_links():
    last = CHAIN - 1
    queue = {}
    for c in range(CHAIN):
        down = [(b, 0, h) for b in range(c, CHAIN) for h in range(PARTS)] + [(last, 1, h) for h in (2, 3)]
        up = [(b, 0, h) for b in range(c, -1, -1) for h in range(PARTS)] + [(0, 1, h) for h in (2, 3)]
        if c > 0:
            queue[c, "down"] = down
        if c < last:
            queue[c, "up"] = up
        near = [b for b in (range(c + 1, CHAIN) if c == 0 else range(c - 1, -1, -1))]
        if c == 1:
            near = [0, 2, 3]
        if c == 2:
            near = [3, 1, 0]
        swap = [(c, 0, h) for h in range(PARTS)]
        for b in near:
            by_chain = (b == last and c < last) or (b == 0 and c > 0)
            swap += [(b, 0, h) for h in range(PARTS) if not (by_chain and h >= 2)]
        queue[c, "swap"] = swap
    have = {(c, (c, 0, h)): 0 for c in range(CHAIN) for h in range(PARTS)}
    start = {key: [] for key in queue}
    for t in range(STEPS):
        new = {}
        for (c, way), items in queue.items():
            at = len(start[c, way])
            if at < len(items) and have.get((c, items[at]), 99) <= t:
                start[c, way].append(t)
                b, sw, h = items[at]
                if way == "swap":
                    new[c, (b, 1 - sw, h)] = t + 1
                else:
                    new[c + (1 if way == "up" else -1), (b, sw, h)] = t + 1
        for key, when in new.items():
            assert key not in have
            have[key] = when
    waits = {(c, t): [] for c in range(CHAIN) for t in range(STEPS)}
    sends = {(c, t): [] for c in range(CHAIN) for t in range(STEPS)}
    for (c, item), when in have.items():
        if when > 0:
            waits[c, when].append(item)
    for (c, way), items in queue.items():
        assert len(start[c, way]) == len(items)
        for item, t in zip(items, start[c, way]):
            ahead = 2 if t < 10 else 1 if t < 12 else 0
            assert have[c, item] < t or t < 12
            sends[c, max(t - ahead, have[c, item], 0)].append((way, item))
    for c in range(CHAIN):
        for k in range(ROUNDS):
            step = [t for t, turns in TURN_AFTER.items() if k in turns][0]
            for b, sw in ARRIVAL[c][k : k + 4]:
                for h in range(PARTS):
                    early = k == ROUNDS - 1 and h in EARLY
                    assert have[c, (b, sw, h)] <= (EARLY_STEP if early else step)
    return waits, sends


def fused_kernel(
    pick_ref, spec_ref, order_ref, table_ref, out_ref,
    blocks, lhs, cross, perm, keep, give, beside, passed, across,
    swap_sem, chain_sem, got_sem, give_sem, beside_sem, passed_sem, across_sem,
):
    nf, _, nw, nc = spec_ref.shape
    part = nf // PARTS
    share = nc // 4
    lag_rows = share * LAGS
    pair = lax.axis_index("pair")
    win = lax.axis_index("win")
    c, x = pair // 2, pair % 2
    row, core = win // 2, win % 2
    swap_to = {"pair": pair + 1 - 2 * x}
    core_to = {"win": win + 1 - 2 * core}
    row_to = {"win": win + 2 - 4 * row}
    waits, sends = plan_links()

    def signal(to):
        pl.semaphore_signal(
            pltpu.get_barrier_semaphore(), inc=1, device_id=to,
            device_id_type=pl.DeviceIdType.MESH,
        )

    signal(swap_to)
    signal(core_to)
    signal(row_to)

    @pl.when(c > 0)
    def _():
        signal({"pair": pair - 2})

    @pl.when(c < CHAIN - 1)
    def _():
        signal({"pair": pair + 2})

    def greet():
        @pl.when((c > 0) & (c < CHAIN - 1))
        def _():
            pl.semaphore_wait(pltpu.get_barrier_semaphore(), 5)

        @pl.when((c == 0) | (c == CHAIN - 1))
        def _():
            pl.semaphore_wait(pltpu.get_barrier_semaphore(), 4)

    def copy(way, item):
        b, sw, h = item
        q = 2 * b + (x if sw == 0 else 1 - x)
        ref = blocks.at[q, pl.ds(h * part, part)]
        if way == "swap":
            sem, to = swap_sem.at[b, h], swap_to
        else:
            side = 0 if way == "down" else 1
            sem = chain_sem.at[side, 2 * b + sw, h]
            to = {"pair": pair - 2 if way == "down" else pair + 2}
        return pltpu.make_async_remote_copy(
            src_ref=ref, dst_ref=ref, send_sem=sem, recv_sem=got_sem.at[q, h],
            device_id=to, device_id_type=pl.DeviceIdType.MESH,
        )

    def links(t, only=None, wait=True, start=True):
        for cs in range(CHAIN):

            @pl.when(c == cs)
            def _(cs=cs):
                if wait and only in (None, 0):
                    for item in waits[cs, t]:
                        copy("swap", item).wait_recv()
                for way, item in sends[cs, t] if start else ():
                    if only is None or item[2] == only:
                        copy(way, item).start()

    def square(f, carry):
        re = spec_ref[f, 0].astype(F32)
        im = spec_ref[f, 1].astype(F32)
        out_ref[pl.ds(pl.multiple_of((f + 2) * nw, 8), nw)] = re * re + im * im
        return carry

    zero = jnp.zeros((nw, nc), F32)
    for edge in (0, 1, nf + 2, nf + 3):
        out_ref[pl.ds(edge * nw, nw)] = zero
    lax.fori_loop(0, part + 2, square, 0, unroll=5)
    rows = lax.broadcasted_iota(jnp.int32, (nc, nc), 0)
    cols = lax.broadcasted_iota(jnp.int32, (nc, nc), 1)
    perm[0] = (rows == order_ref[...]).astype(F32).astype(BF)
    perm[1] = (rows == cols).astype(F32).astype(BF)

    def scale(f, carry):
        total = out_ref[pl.ds(pl.multiple_of(f * nw, 8), nw)]
        for d in range(1, 5):
            total += out_ref[pl.ds(pl.multiple_of((f + d) * nw, 8), nw)]
        count = jnp.minimum(f + 2, nf - 1) - jnp.maximum(f - 2, 0) + 1
        mean = total / count.astype(F32)
        inv = 1.0 / jnp.maximum(jnp.sqrt(mean), 0.5)
        white = jnp.concatenate(
            [
                (spec_ref[f, 0].astype(F32) * inv).astype(BF),
                (spec_ref[f, 1].astype(F32) * inv).astype(BF),
            ],
            0,
        )
        blocks[pair, f] = jnp.dot(white, perm[0], preferred_element_type=F32).astype(BF)
        return carry

    greet()
    for h in range(PARTS):
        lax.fori_loop(h * part, (h + 1) * part, scale, 0, unroll=4)
        links(0, h)
        if h == 0:
            lax.fori_loop(part + 2, nf, square, 0, unroll=2)

    def turn_bin(f, carry):
        turned = lax.dot_general(
            perm[1], blocks[pair, f], (((1,), (1,)), ((), ())), preferred_element_type=F32
        )
        lhs[f] = turned.astype(BF)
        return carry

    lax.fori_loop(0, nf, turn_bin, 0, unroll=4)

    piece_rows = lag_rows // 2

    def to_core(k, half, piece):
        at = pl.ds(half * lag_rows + piece * piece_rows, piece_rows)
        return pltpu.make_async_remote_copy(
            src_ref=give.at[k % 2, at], dst_ref=beside.at[k, at],
            send_sem=give_sem.at[k, half, piece], recv_sem=beside_sem.at[k, half, piece],
            device_id=core_to, device_id_type=pl.DeviceIdType.MESH,
        )

    def to_row(k, piece):
        at = pl.ds(piece * piece_rows, piece_rows)
        return pltpu.make_async_remote_copy(
            src_ref=passed.at[k, at], dst_ref=across.at[k, at],
            send_sem=passed_sem.at[k, piece], recv_sem=across_sem.at[k, piece],
            device_id=row_to, device_id_type=pl.DeviceIdType.MESH,
        )

    def cross_turn(k, parts):
        places = []
        for m in range(4):
            at = jnp.int32(0)
            for cs in range(CHAIN):
                b, sw = ARRIVAL[cs][k + m]
                at = at + (c == cs).astype(jnp.int32) * (2 * b + (x if sw == 0 else 1 - x))
            places.append(at)

        def one_bin(f, carry):
            right = None
            for m in range(4):
                weight = (pick_ref[k] == m).astype(F32)
                term = blocks[places[m], f] * jnp.full((1, nc), weight, F32).astype(BF)
                right = term if right is None else right + term
            turned = jnp.concatenate([right[nw:], -right[:nw]], 0)
            left = lhs[f]
            cross[f] = jnp.dot(left, right, preferred_element_type=F32).astype(BF)
            cross[nf + f] = jnp.dot(left, turned, preferred_element_type=F32).astype(BF)
            return carry

        for h in parts:
            lax.fori_loop(h * part, (h + 1) * part, one_bin, 0, unroll=4)

    def lag_turn(k):
        if k >= 2:
            for half in range(2):
                for piece in range(2):
                    to_core(k - 2, half, piece).wait_send()

        def lags_of(half, other, u):
            owner = lax.rem(row + half, 2) * 2 + lax.rem(core + other, 2)
            start = pl.multiple_of(owner * share + u * GROUP, GROUP)
            right = cross[:, pl.ds(start, GROUP), :].reshape(2 * nf * GROUP, nc)
            return jnp.dot(table_ref[...], right, preferred_element_type=F32)

        size = GROUP * LAGS

        def send_group(half, u, carry):
            at = pl.multiple_of(half * lag_rows + u * size, size)
            give[k % 2, pl.ds(at, size)] = lags_of(half, 1, u).astype(BF)
            return carry

        def keep_group(half, u, carry):
            if half == 1:
                keep[pl.ds(pl.multiple_of(u * size, size), size)] = lags_of(1, 0, u)
            else:
                to = pl.multiple_of(k * lag_rows + u * size, size)
                out_ref[pl.ds(to, size)] = lags_of(0, 0, u)
            return carry

        groups = share // GROUP // 2

        def receive(half, piece):
            to_core(k, half, piece).wait_recv()
            at = half * lag_rows + piece * piece_rows
            return beside[k, pl.ds(at, piece_rows)].astype(F32)

        for half in (1, 0):
            for piece in range(2):
                first, last = piece * groups, (piece + 1) * groups
                lax.fori_loop(first, last, functools.partial(send_group, half), 0, unroll=2)
                to_core(k, half, piece).start()
                lax.fori_loop(first, last, functools.partial(keep_group, half), 0, unroll=2)
                if half == 1:
                    at = pl.ds(piece * piece_rows, piece_rows)
                    passed[k, at] = (keep[at] + receive(half, piece)).astype(BF)
                    to_row(k, piece).start()
        for piece in range(2):
            at = pl.ds(k * lag_rows + piece * piece_rows, piece_rows)
            out_ref[at] += receive(0, piece)

    for t in range(1, STEPS):
        links(t, start=t != EARLY_STEP)
        for k in TURN_AFTER.get(t, ()):
            if k == 2:
                links(EARLY_STEP, wait=False)
            late = k == ROUNDS - 1
            cross_turn(k, [h for h in range(PARTS) if not (late and h in EARLY)])
            lag_turn(k)
        if t == EARLY_STEP:
            cross_turn(ROUNDS - 1, EARLY)
    for k in range(ROUNDS):
        for piece in range(2):
            to_row(k, piece).wait_recv()
            at = pl.ds(k * lag_rows + piece * piece_rows, piece_rows)
            out_ref[at] += across[k, pl.ds(piece * piece_rows, piece_rows)].astype(F32)
    for k in range(ROUNDS):
        for piece in range(2):
            if k >= 2:
                for half in range(2):
                    to_core(k, half, piece).wait_send()
            to_row(k, piece).wait_send()
    for cs in range(CHAIN):

        @pl.when(c == cs)
        def _(cs=cs):
            for t in range(STEPS):
                for way, item in sends[cs, t]:
                    copy(way, item).wait_send()


def fused(pick, spectra, order, table):
    nf, _, nw, nc = spectra.shape
    blocks = lax.axis_size("pair")
    rows = nc // 4 * LAGS
    vmem = pl.BlockSpec(memory_space=pltpu.VMEM)
    dma = pltpu.SemaphoreType.DMA
    return pl.pallas_call(
        fused_kernel,
        out_shape=jax.ShapeDtypeStruct((ROUNDS * rows, nc), F32),
        in_specs=[pl.BlockSpec(memory_space=pltpu.SMEM), vmem, vmem, vmem],
        out_specs=vmem,
        scratch_shapes=[
            pltpu.VMEM((blocks, nf, 2 * nw, nc), BF),
            pltpu.VMEM((nf, nc, 2 * nw), BF),
            pltpu.VMEM((2 * nf, nc, nc), BF),
            pltpu.VMEM((2, nc, nc), BF),
            pltpu.VMEM((rows, nc), F32),
            pltpu.VMEM((2, 2 * rows, nc), BF),
            pltpu.VMEM((ROUNDS, 2 * rows, nc), BF),
            pltpu.VMEM((ROUNDS, rows, nc), BF),
            pltpu.VMEM((ROUNDS, rows, nc), BF),
            dma((CHAIN, PARTS)),
            dma((2, 2 * CHAIN, PARTS)),
            dma((blocks, PARTS)),
            dma((ROUNDS, 2, 2)),
            dma((ROUNDS, 2, 2)),
            dma((ROUNDS, 2)),
            dma((ROUNDS, 2)),
        ],
        cost_estimate=pl.CostEstimate(
            flops=16_000_000_000, bytes_accessed=16_000_000, transcendentals=0
        ),
        compiler_params=pltpu.CompilerParams(
            vmem_limit_bytes=60 * 2**20, collective_id=0, has_side_effects=True
        ),
        name="fused",
    )(pick, spectra, order, table)


def arrange_kernel(place_ref, sums_ref, out_ref, held, in_sem, out_sem):
    rounds, rows = held.shape[:2]
    half = rows // 2
    for r in range(rounds):
        for h in range(2):
            at = pl.ds(h * half, half)
            pltpu.make_async_copy(
                sums_ref.at[place_ref[r], at], held.at[r, at], in_sem.at[r, h]
            ).start()
    for step in ("move", "finish"):
        for r in range(rounds):
            for h in range(2):
                at = pl.ds(h * half, half)
                out = pltpu.make_async_copy(held.at[r, at], out_ref.at[at, r], out_sem.at[r, h])
                if step == "move":
                    pltpu.make_async_copy(
                        sums_ref.at[place_ref[r], at], held.at[r, at], in_sem.at[r, h]
                    ).wait()
                    out.start()
                else:
                    out.wait()


def arrange(place, sums):
    rounds, rows, lags, nc = sums.shape
    return pl.pallas_call(
        arrange_kernel,
        in_specs=[
            pl.BlockSpec(memory_space=pltpu.SMEM),
            pl.BlockSpec(memory_space=pl.ANY),
        ],
        out_specs=pl.BlockSpec(memory_space=pl.ANY),
        out_shape=jax.ShapeDtypeStruct((rows, rounds, lags, nc), F32),
        scratch_shapes=[
            pltpu.VMEM((rounds, rows, lags, nc), F32),
            pltpu.SemaphoreType.DMA((rounds, 2)),
            pltpu.SemaphoreType.DMA((rounds, 2)),
        ],
        name="arrange",
    )(place, sums)


def local(spectra, channel_order, partners):
    num_blocks = lax.axis_size("pair")
    win_count = lax.axis_size("win")
    nf, _, nw, nc = spectra.shape
    spread = jnp.asarray(make_table(nf, LAGS, nw * win_count))
    me = lax.axis_index("pair")
    win = lax.axis_index("win")
    if num_blocks == 2 * CHAIN and win_count == 4:
        mine = partners[:, me]
        rank = jnp.zeros_like(mine)
        for c in range(CHAIN):
            for index, (b, sw) in enumerate(ARRIVAL[c]):
                same = (mine // 2 == b) & ((mine % 2 != me % 2) == (sw == 1))
                rank = jnp.where((me // 2 == c) & same, index, rank)
        place = jnp.sum((rank[None, :] < rank[:, None]).astype(jnp.int32), 1)
        turns = jnp.arange(ROUNDS, dtype=jnp.int32)
        pick = jnp.sum(jnp.where(place[None, :] == turns[:, None], rank[None, :], 0), 1) - turns
        sums = fused(pick.astype(jnp.int32), spectra, channel_order, spread)
        return arrange(place, sums.reshape(ROUNDS, nc // 4, LAGS, nc))[None]
    own, lhs = whiten(spectra, channel_order)
    row, core = win // 2, win % 2
    results = []
    turned = lax.all_to_all(
        own.reshape(num_blocks, -1), "pair", split_axis=0, concat_axis=0, tiled=True
    )
    for turn in range(ROUNDS):
        arranged = jnp.take(turned, partners[turn], axis=0)
        received = lax.all_to_all(arranged, "pair", split_axis=0, concat_axis=0, tiled=True)
        info = jnp.stack([jnp.int32(0), core, row]).astype(jnp.int32)
        keep, give = correlate(info, lhs, spread, [received.reshape(own.shape)])
        beside = lax.ppermute(give, "win", [(w, w ^ 1) for w in range(win_count)])
        passed = (keep[1] + beside[1].astype(F32)).astype(BF)
        across = lax.ppermute(passed, "win", [(w, w ^ 2) for w in range(win_count)])
        results.append(keep[0] + beside[0].astype(F32) + across.astype(F32))
    return jnp.stack(results, 1)[None]


def solution(mesh):
    return jax.shard_map(
        local,
        mesh=mesh,
        in_specs=(P(None, None, "win", "pair"), P("pair", None), P()),
        out_specs=P("pair", "win", None, None, None),
        check_vma=False,
    )
```
